32 devices in a mesh: group: 2 (over x), replica: 16 (over z, y, core).
Axes of the slice: x: 2, y: 2, z: 4, core: 2. Of those that a mesh axis runs over, the one named last changes fastest.
Arguments:
- hidden: bfloat16 [256, 8192], P(('group', 'replica')), parts along dimension 0, may hold values from -6 to 6
- input_norm_gain: float32 [8192], replicated, may hold values from 0.1 to 1.9
- row_adapter_index: int32 [256, 1], P(('group', 'replica')), parts along dimension 0, may hold values from 0 to 15; in each aligned block of 128 rows (0 to 127, 128 to 255, ...) at most 16 rows name the same one
- adapter_slot_table: int32 [16], replicated, may hold values from 0 to 15, each once
- cache_length: int32 [256], P(('group', 'replica')), parts along dimension 0, may hold values from 1 to 96, as said below
- rotated_key_cache: bfloat16 [256, 96, 1024], P(('group', 'replica')), parts along dimension 0, may hold values from -480 to 480
- cached_value_table: bfloat16 [256, 96, 1024], P(('group', 'replica')), parts along dimension 0, may hold values from -6 to 6
- query_weight: bfloat16 [8192, 8192], P(None, 'replica'), may hold values from -0.0625 to 0.0625
- key_value_weight: bfloat16 [2, 1024, 8192], P(None, 'replica'), may hold values from -0.0625 to 0.0625
- output_weight: bfloat16 [8192, 8192], P(None, 'replica'), may hold values from -0.25 to 0.25
- adapter_down_weight: bfloat16 [16, 4, 64, 8192], P('replica'), may hold values from -0.0625 to 0.0625
- query_up_weight: bfloat16 [16, 64, 8192], P('replica'), may hold values from -0.75 to 0.75
- key_value_up_weight: bfloat16 [16, 2, 64, 1024], P('replica'), may hold values from -0.75 to 0.75
- output_up_weight: bfloat16 [16, 64, 8192], P('replica'), may hold values from -0.75 to 0.75
Outputs:
- attn_out: bfloat16 [256, 8192], P(('group', 'replica')), parts along dimension 0
The draws below stay inside these ranges and needn't reach their ends.
There are 2 independent parts, one for each index of `group`. The reference program is written for one: setup_inputs(seed, part) draws one part's arguments, and reference() takes and returns one part's arrays. A program takes and returns all parts, laid end to end along the dimension named above; an argument that names none is the same for every part. Nothing has to cross between parts.
Inputs may be any that keep to these rules, and one draw needn't show every extreme that they name: `row_adapter_index`: no adapter is named by more than 16 of the 128 rows of a group. `adapter_slot_table`: each slot once. `cache_length`: among the rows of each replica one has length 96.
All inputs are finite; a program needn't handle non-finite values.
Results may differ from the reference program's by a relative error of at most 0.0075.
The reference program's roundings to bfloat16 on the way count: a program that leaves them out, or rounds other values in their place, can miss the bound.
Values may be sent and summed in bfloat16 or wider, within the bound.
A program may use at most 128 MiB of HBM per device.

```python
import math
import jax
import jax.numpy as jnp
import numpy as np
from jax import lax

MODEL_WIDTH = 8192
HEADS = 64
KV_HEADS = 8
HD = 128
ADAPTER_RANK = 64
TOK_DEV = 8
LENGTH = 96
ROWS = 128
ADAPTER_COUNT = 16
CAPACITY = 16


def draw_cache_length(key, part):
    key = jax.random.fold_in(key, 17)
    first, second = jax.random.split(key)
    lengths = jax.random.randint(first, (ROWS,), 1, LENGTH + 1)
    chosen = jax.random.randint(second, (ROWS // TOK_DEV, 1), 0, TOK_DEV)
    longest = jnp.arange(ROWS).reshape(ROWS // TOK_DEV, TOK_DEV) == chosen
    return jnp.where(longest.reshape(ROWS), LENGTH, lengths).astype(jnp.int32)


def draw_rotated_key_cache(key, part):
    key = jax.random.fold_in(key, 29)
    first = jax.random.fold_in(key, 0)
    values = jnp.clip(jax.random.normal(first, (ROWS, LENGTH, KV_HEADS * HD), jnp.float32), -6.0, 6.0)
    return values.astype(jnp.bfloat16)


def levels(stream_key, dims, cuts, low, top_value):
    def one(dim, blocks):
        draws = jax.random.uniform(jax.random.fold_in(jax.random.fold_in(stream_key, 6), dim), (blocks,), jnp.float32, low / len(cuts), top_value / len(cuts))
        return jnp.repeat(jnp.exp(draws), dims[dim] // blocks).reshape((-1,) + (1,) * (len(dims) - dim - 1))

    level = one(*cuts[0])
    for cut in cuts[1:]:
        level = level * one(*cut)
    return level


def deal_out(stream_key, own, number, rows, amount, top, most, lean):
    order = jax.random.permutation(stream_key, amount)
    crowded, usual = shares(amount, rows * top, most, lean, True), shares(amount, rows * top, most, lean, False)
    places = jnp.arange(amount)

    def named(tallies, offset_by):
        used = int((tallies > 0).sum())
        fixed = max(1, used // 4)
        passed = fixed + (places - fixed + offset_by * (used - fixed)) % max(1, amount - fixed)
        return jnp.zeros((amount,), jnp.int32).at[order[jnp.where(places < fixed, places, passed)]].set(jnp.asarray(tallies, jnp.int32))

    tallies = jnp.where(number % 4 == 0, named(crowded, number // 4), named(usual, number - number // 4 - 1))
    mixed = jax.random.permutation(jax.random.fold_in(own, 3), amount)
    giver, receiver = mixed[0:amount // 2 * 2:2], mixed[1:amount // 2 * 2:2]
    slack = jnp.minimum(tallies[giver] - 1, most - tallies[receiver]) // 2
    slack = jnp.where((giver == order[0]) | (receiver == order[0]) | (tallies[receiver] == 0), 0, jnp.maximum(slack, 0))
    passed = jax.random.randint(jax.random.fold_in(own, 4), (amount // 2,), 0, 1 << 20) % (slack + 1)
    tallies = tallies.at[giver].add(-passed).at[receiver].add(passed)
    labels = jnp.searchsorted(jnp.cumsum(tallies), jnp.arange(rows * top), side="right").astype(jnp.int32)
    listing = labels.reshape(top, rows).T
    listing = listing[jax.random.permutation(jax.random.fold_in(own, 1), rows)]
    offset_by = jax.random.randint(jax.random.fold_in(own, 2), (rows, 1), 0, top)
    return jnp.take_along_axis(listing, (jnp.arange(top)[None, :] + offset_by) % top, axis=1)


def shares(number_of, total, bound, lean, full):
    loads = [(1 << 20) // math.isqrt(grade ** lean) + 1 for grade in range(1, number_of + 1)]
    largest = bound if full else min(bound, max(-(-total // number_of), total * loads[0] // sum(loads)))
    least = 1 if total - largest >= number_of - 1 else 0
    holding, surplus = [largest] + [least] * (number_of - 1), total - largest - least * (number_of - 1)
    while surplus > 0:
        movable = [i for i in range(1, number_of) if holding[i] < largest] or [i for i in range(1, number_of) if holding[i] < bound]
        mass, left = sum([loads[i] for i in movable]), surplus
        for i in movable:
            more = min(bound - holding[i], max(1, left * loads[i] // mass), surplus)
            holding[i] = holding[i] + more
            surplus = surplus - more
    return np.array(holding)


def bell_draw(stream_key, shape, spread, reach, cuts=(), kind=jnp.bfloat16):
    factor_of = levels(stream_key, shape, cuts, -0.22, 0.18) if cuts else 1.0
    result = jax.random.normal(stream_key, shape, jnp.float32) * spread * factor_of
    return jnp.minimum(jnp.maximum(result, -reach), reach).astype(kind)


def setup_inputs(seed: int = 0, part: int = 0) -> dict:
    splits = jax.random.split(jax.random.key(seed), 15)
    part_keys = jax.random.split(jax.random.fold_in(splits[14], part), 15)
    hidden = bell_draw(part_keys[0], (ROWS, MODEL_WIDTH), 1.0, 6.0, ((0, 16),))
    input_norm_gain = jnp.clip(1.0 + 0.18 * jax.random.normal(splits[1], (MODEL_WIDTH,), jnp.float32), 0.1, 1.9)
    row_adapter_index_keys = jax.random.split(jax.random.fold_in(part_keys[2], 1), ROWS // ROWS)
    row_adapter_index_turns = jax.random.permutation(jax.random.fold_in(part_keys[2], 3), ROWS // ROWS)
    row_adapter_index = jax.vmap(lambda own, number: deal_out(jax.random.fold_in(part_keys[2], 2), own, number, ROWS, ADAPTER_COUNT, 1, CAPACITY, 2))(row_adapter_index_keys, row_adapter_index_turns).reshape((ROWS, 1))
    adapter_slot_table = jax.random.permutation(splits[3], ADAPTER_COUNT).astype(jnp.int32)
    cache_length = draw_cache_length(jax.random.fold_in(jax.random.fold_in(splits[14], part), 71), part)
    rotated_key_cache = draw_rotated_key_cache(jax.random.fold_in(jax.random.fold_in(splits[14], part), 71), part)
    cached_value_table = bell_draw(part_keys[6], (ROWS, LENGTH, KV_HEADS * HD), 1.0, 6.0, ((0, 16),))
    query_weight = bell_draw(splits[7], (MODEL_WIDTH, HEADS * HD), MODEL_WIDTH ** -0.5, 0.0625, ((1, 16),))
    key_value_weight = bell_draw(splits[8], (2, KV_HEADS * HD, MODEL_WIDTH), MODEL_WIDTH ** -0.5, 0.0625, ((1, 16),))
    output_weight = bell_draw(splits[9], (HEADS * HD, MODEL_WIDTH), (4 * HD) ** -0.5, 0.25, ((1, 16),))
    adapter_down_weight = bell_draw(splits[10], (ADAPTER_COUNT, 4, ADAPTER_RANK, MODEL_WIDTH), MODEL_WIDTH ** -0.5, 0.0625, ((0, 16),))
    query_up_weight = bell_draw(splits[11], (ADAPTER_COUNT, ADAPTER_RANK, HEADS * HD), ADAPTER_RANK ** -0.5, 0.75, ((0, 16),))
    key_value_up_weight = bell_draw(splits[12], (ADAPTER_COUNT, 2, ADAPTER_RANK, KV_HEADS * HD), ADAPTER_RANK ** -0.5, 0.75, ((0, 16),))
    output_up_weight = bell_draw(splits[13], (ADAPTER_COUNT, ADAPTER_RANK, MODEL_WIDTH), ADAPTER_RANK ** -0.5, 0.75, ((0, 16),))
    return {"hidden": hidden, "input_norm_gain": input_norm_gain, "row_adapter_index": row_adapter_index, "adapter_slot_table": adapter_slot_table, "cache_length": cache_length, "rotated_key_cache": rotated_key_cache, "cached_value_table": cached_value_table, "query_weight": query_weight, "key_value_weight": key_value_weight, "output_weight": output_weight, "adapter_down_weight": adapter_down_weight, "query_up_weight": query_up_weight, "key_value_up_weight": key_value_up_weight, "output_up_weight": output_up_weight}


adapter_scale = 0.5

def rms_norm(hidden, input_norm_gain):
    values = hidden.astype(jnp.float32)
    scaled = values * lax.rsqrt(lax.optimization_barrier(jnp.mean(values * values, axis=-1, keepdims=True)) + 1e-06)
    return (scaled * input_norm_gain.astype(jnp.float32)).astype(jnp.bfloat16)

def rotate(values, position):
    half_width = HD // 2
    inv_freq = 1000000.0 ** (-(jnp.arange(half_width, dtype=jnp.float32) * 2.0 / HD))
    angles = position.astype(jnp.float32)[:, None, None] * inv_freq[None, None, :]
    cosine = jnp.concatenate([jnp.cos(angles), jnp.cos(angles)], axis=-1)
    sine_part = jnp.concatenate([jnp.sin(angles), jnp.sin(angles)], axis=-1)
    rotated = jnp.concatenate([-values[..., half_width:], values[..., :half_width]], axis=-1)
    return values * cosine + rotated * sine_part

def attend(queries, new_keys, new_values, cache_length, rotated_key_cache, cached_value_table):
    row_count = queries.shape[0]
    groups = HEADS // KV_HEADS
    scale_factor = 1.0 / math.sqrt(HD)
    heads_q = rotate(queries.astype(jnp.float32).reshape(row_count, HEADS, HD), cache_length).astype(jnp.bfloat16)
    heads_k = rotate(new_keys.astype(jnp.float32).reshape(row_count, KV_HEADS, HD), cache_length).astype(jnp.bfloat16)
    grouped_q = heads_q.astype(jnp.float32).reshape(row_count, KV_HEADS, groups, HD)
    cached_k = rotated_key_cache.astype(jnp.float32).reshape(row_count, LENGTH, KV_HEADS, HD)
    cached_v = cached_value_table.astype(jnp.float32).reshape(row_count, LENGTH, KV_HEADS, HD)
    scores = jnp.einsum('rgjd,rtgd->rgjt', grouped_q, cached_k) * scale_factor
    own_score = jnp.einsum('rgjd,rgd->rgj', grouped_q, heads_k.astype(jnp.float32)) * scale_factor
    visible = (jnp.arange(LENGTH)[None, :] < cache_length[:, None])[:, None, None, :]
    masked = jnp.where(visible, scores, -1e+30)
    largest = jnp.maximum(lax.optimization_barrier(jnp.max(masked, axis=-1)), own_score)
    weights = jnp.where(visible, jnp.exp(masked - largest[..., None]), 0.0)
    own_weight = jnp.exp(own_score - largest)
    denominator = lax.optimization_barrier(jnp.sum(weights, axis=-1)) + own_weight
    chances = (weights / denominator[..., None]).astype(jnp.bfloat16)
    own_chance = (own_weight / denominator).astype(jnp.bfloat16)
    mixed_values = jnp.einsum('rgjt,rtgd->rgjd', chances.astype(jnp.float32), cached_v)
    mixed_values = mixed_values + own_chance.astype(jnp.float32)[..., None] * new_values.astype(jnp.float32).reshape(row_count, KV_HEADS, 1, HD)
    return mixed_values.reshape(row_count, HEADS * HD).astype(jnp.bfloat16)

def down_weight_rows(value_row_list, owner_devices, adapter_down_weight, selected_adapter):

    def single(key_value_pair):
        return jnp.dot(adapter_down_weight[key_value_pair[1], selected_adapter], key_value_pair[0], preferred_element_type=jnp.float32)
    return lax.map(single, (value_row_list, owner_devices)).astype(jnp.bfloat16)

def up_weight_rows(factor_list, owner_devices, table):

    def single(key_value_pair):
        return jnp.dot(key_value_pair[0], table[key_value_pair[1]], preferred_element_type=jnp.float32)
    return lax.map(single, (factor_list, owner_devices))

def reference(hidden, input_norm_gain, row_adapter_index, adapter_slot_table, cache_length, rotated_key_cache, cached_value_table, query_weight, key_value_weight, output_weight, adapter_down_weight, query_up_weight, key_value_up_weight, output_up_weight):
    normalized_input = rms_norm(hidden, input_norm_gain)
    owner_devices = adapter_slot_table[row_adapter_index[:, 0]].astype(jnp.int32)
    queries = jnp.dot(normalized_input, query_weight, preferred_element_type=jnp.float32)
    key_new = jnp.dot(normalized_input, key_value_weight[0].T, preferred_element_type=jnp.float32)
    value_new = jnp.dot(normalized_input, key_value_weight[1].T, preferred_element_type=jnp.float32)
    query_factor = down_weight_rows(normalized_input, owner_devices, adapter_down_weight, 0)
    key_factor = down_weight_rows(normalized_input, owner_devices, adapter_down_weight, 1)
    value_factor = down_weight_rows(normalized_input, owner_devices, adapter_down_weight, 2)
    query_update = (adapter_scale * up_weight_rows(query_factor, owner_devices, query_up_weight)).astype(jnp.bfloat16)
    key_update = (adapter_scale * up_weight_rows(key_factor, owner_devices, key_value_up_weight[:, 0])).astype(jnp.bfloat16)
    value_update = (adapter_scale * up_weight_rows(value_factor, owner_devices, key_value_up_weight[:, 1])).astype(jnp.bfloat16)
    q_full = (queries + query_update.astype(jnp.float32)).astype(jnp.bfloat16)
    k_full = (key_new + key_update.astype(jnp.float32)).astype(jnp.bfloat16)
    v_full = (value_new + value_update.astype(jnp.float32)).astype(jnp.bfloat16)
    attention_result = attend(q_full, k_full, v_full, cache_length, rotated_key_cache, cached_value_table)
    output_factor_rows = down_weight_rows(attention_result, owner_devices, adapter_down_weight, 3)
    layer_output = jnp.dot(attention_result, output_weight, preferred_element_type=jnp.float32) + adapter_scale * up_weight_rows(output_factor_rows, owner_devices, output_up_weight)
    return layer_output.astype(jnp.bfloat16)
```

```python
import functools
import math

import jax
import jax.numpy as jnp
from jax import lax
from jax.experimental import pallas as pl
from jax.experimental.pallas import tpu as pltpu
from jax.sharding import PartitionSpec as P

HEADS = 64
KV_HEADS = 8
HD = 128
LENGTH = 96


adapter_scale = 0.5


def rms_norm(hidden, input_norm_gain):
    values = hidden.astype(jnp.float32)
    scaled = values * lax.rsqrt(jnp.mean(values * values, axis=-1, keepdims=True) + 1e-06)
    return (scaled * input_norm_gain).astype(jnp.bfloat16)


def rotate(values, position):
    half_width = HD // 2
    inv_freq = 1000000.0 ** (-(jnp.arange(half_width, dtype=jnp.float32) * 2.0 / HD))
    angles = position.astype(jnp.float32)[:, None, None] * inv_freq[None, None, :]
    cosine = jnp.concatenate([jnp.cos(angles), jnp.cos(angles)], axis=-1)
    sine_part = jnp.concatenate([jnp.sin(angles), jnp.sin(angles)], axis=-1)
    rotated = jnp.concatenate([-values[..., half_width:], values[..., :half_width]], axis=-1)
    return values * cosine + rotated * sine_part


def attend(queries, new_keys, new_values, cache_length, rotated_key_cache, cached_value_table):
    row_count = queries.shape[0]
    groups = HEADS // KV_HEADS
    scale_factor = 1.0 / math.sqrt(HD)
    heads_q = rotate(
        queries.astype(jnp.float32).reshape(row_count, HEADS, HD), cache_length
    ).astype(jnp.bfloat16)
    heads_k = rotate(
        new_keys.astype(jnp.float32).reshape(row_count, KV_HEADS, HD), cache_length
    ).astype(jnp.bfloat16)
    grouped_q = heads_q.reshape(row_count, KV_HEADS, groups, HD)
    cached_k = rotated_key_cache.reshape(row_count, LENGTH, KV_HEADS, HD)
    cached_v = cached_value_table.reshape(row_count, LENGTH, KV_HEADS, HD)
    scores = (
        jnp.einsum("rgjd,rtgd->rgjt", grouped_q, cached_k, preferred_element_type=jnp.float32)
        * scale_factor
    )
    own_score = (
        jnp.einsum("rgjd,rgd->rgj", grouped_q, heads_k, preferred_element_type=jnp.float32)
        * scale_factor
    )
    visible = (jnp.arange(LENGTH)[None, :] < cache_length[:, None])[:, None, None, :]
    masked = jnp.where(visible, scores, -1e30)
    largest = jnp.maximum(jnp.max(masked, axis=-1), own_score)
    weights = jnp.where(visible, jnp.exp(masked - largest[..., None]), 0.0)
    own_weight = jnp.exp(own_score - largest)
    denominator = jnp.sum(weights, axis=-1) + own_weight
    chances = (weights / denominator[..., None]).astype(jnp.bfloat16)
    own_chance = (own_weight / denominator).astype(jnp.bfloat16)
    mixed_values = jnp.einsum(
        "rgjt,rtgd->rgjd", chances, cached_v, preferred_element_type=jnp.float32
    )
    mixed_values = mixed_values + own_chance.astype(jnp.float32)[..., None] * new_values.astype(
        jnp.float32
    ).reshape(row_count, KV_HEADS, 1, HD)
    return mixed_values.reshape(row_count, HEADS * HD).astype(jnp.bfloat16)


def local(
    hidden,
    input_norm_gain,
    row_adapter_index,
    adapter_slot_table,
    cache_length,
    rotated_key_cache,
    cached_value_table,
    query_weight,
    key_value_weight,
    output_weight,
    adapter_down_weight,
    query_up_weight,
    key_value_up_weight,
    output_up_weight,
):
    devices = lax.axis_size("replica")
    myself = lax.axis_index("replica")
    local_rows = hidden.shape[0]
    capacity = 2 * local_rows
    adapters = adapter_slot_table.shape[0]
    normalized_input = rms_norm(hidden, input_norm_gain)
    picked = (row_adapter_index == jnp.arange(adapters)[None, :]).astype(jnp.int32)
    owner_devices = jnp.sum(picked * adapter_slot_table[None, :], axis=1)
    all_normed, all_owners = (
        lax.all_gather(normalized_input, "replica", axis=0, tiled=True),
        lax.all_gather(owner_devices, "replica", axis=0, tiled=True),
    )
    member = (all_owners[:, None] == jnp.arange(devices)[None, :]).astype(jnp.int32)
    running = jnp.cumsum(member, axis=0)
    position = all_owners * capacity + jnp.sum(running * member, axis=1) - 1
    my_slots = myself * capacity + jnp.arange(capacity)
    select = (position[None, :] == my_slots[:, None]).astype(jnp.bfloat16)
    my_rows = jnp.dot(select, all_normed, preferred_element_type=jnp.float32).astype(jnp.bfloat16)
    down_weight_maps = adapter_down_weight[0]
    factor_list = jnp.einsum(
        "cd,prd->cpr", my_rows, down_weight_maps[:3], preferred_element_type=jnp.float32
    ).astype(jnp.bfloat16)
    query_update = (
        adapter_scale
        * jnp.dot(factor_list[:, 0], query_up_weight[0], preferred_element_type=jnp.float32)
    ).astype(jnp.bfloat16)
    key_update = (
        adapter_scale
        * jnp.dot(factor_list[:, 1], key_value_up_weight[0, 0], preferred_element_type=jnp.float32)
    ).astype(jnp.bfloat16)
    value_update = (
        adapter_scale
        * jnp.dot(factor_list[:, 2], key_value_up_weight[0, 1], preferred_element_type=jnp.float32)
    ).astype(jnp.bfloat16)
    slot_q, slot_k, slot_v = (
        lax.all_to_all(query_update, "replica", split_axis=1, concat_axis=0, tiled=True),
        lax.all_to_all(key_update, "replica", split_axis=1, concat_axis=0, tiled=True),
        lax.all_to_all(value_update, "replica", split_axis=1, concat_axis=0, tiled=True),
    )
    contract = (((1,), (1,)), ((), ()))
    queries = jnp.dot(all_normed, query_weight, preferred_element_type=jnp.float32) + jnp.take(
        slot_q, position, axis=0
    ).astype(jnp.float32)
    key_new = lax.dot_general(
        all_normed, key_value_weight[0], contract, preferred_element_type=jnp.float32
    ) + jnp.take(slot_k, position, axis=0).astype(jnp.float32)
    value_new = lax.dot_general(
        all_normed, key_value_weight[1], contract, preferred_element_type=jnp.float32
    ) + jnp.take(slot_v, position, axis=0).astype(jnp.float32)
    q_rows, k_rows, v_rows = (
        lax.all_to_all(
            queries.astype(jnp.bfloat16), "replica", split_axis=0, concat_axis=1, tiled=True
        ),
        lax.all_to_all(
            key_new.astype(jnp.bfloat16), "replica", split_axis=0, concat_axis=1, tiled=True
        ),
        lax.all_to_all(
            value_new.astype(jnp.bfloat16), "replica", split_axis=0, concat_axis=1, tiled=True
        ),
    )
    attention_result = attend(
        q_rows, k_rows, v_rows, cache_length, rotated_key_cache, cached_value_table
    )
    attended_all = lax.all_gather(attention_result, "replica", axis=0, tiled=True)
    my_attended = jnp.dot(select, attended_all, preferred_element_type=jnp.float32).astype(
        jnp.bfloat16
    )
    output_factor = lax.dot_general(
        my_attended, down_weight_maps[3], contract, preferred_element_type=jnp.float32
    ).astype(jnp.bfloat16)
    output_update = adapter_scale * jnp.dot(
        output_factor, output_up_weight[0], preferred_element_type=jnp.float32
    )
    delta_cols = lax.all_to_all(
        output_update.astype(jnp.bfloat16), "replica", split_axis=1, concat_axis=0, tiled=True
    ).astype(output_update.dtype)
    partial_cols = jnp.dot(
        attended_all, output_weight, preferred_element_type=jnp.float32
    ) + jnp.take(delta_cols, position, axis=0)
    return lax.all_to_all(
        partial_cols.astype(jnp.bfloat16), "replica", split_axis=0, concat_axis=1, tiled=True
    )


CHUNKS = 4
Z_STRIDE = 4
Z_COUNT = 4


def remote(source, target, send_sem, recv_sem, device):
    return pltpu.make_async_remote_copy(
        src_ref=source,
        dst_ref=target,
        send_sem=send_sem,
        recv_sem=recv_sem,
        device_id={"replica": device},
        device_id_type=pl.DeviceIdType.MESH,
    )


def greet_all(devices, me):
    barrier = pltpu.get_barrier_semaphore()

    def greet(i, carry):
        pl.semaphore_signal(
            barrier,
            inc=1,
            device_id={"replica": (me + i) % devices},
            device_id_type=pl.DeviceIdType.MESH,
        )
        return carry

    lax.fori_loop(1, devices, greet, 0)
    pl.semaphore_wait(barrier, devices - 1)


class Gather:
    def __init__(self, devices, me, blocks, send_sem, recv_sem):
        self.devices, self.me, self.blocks = devices, me, blocks
        self.send_sem, self.recv_sem = send_sem, recv_sem
        self.y_peer = me + 2 - 4 * ((me // 2) % 2)
        self.core_peer = me + 1 - 2 * (me % 2)

    def copy(self, k, origin, device, number):
        block = self.blocks.at[k, origin]
        return remote(
            block, block, self.send_sem.at[k, number], self.recv_sem.at[k, origin], device
        )

    def own(self, k):
        for i in range(1, Z_COUNT):
            self.copy(k, self.me, (self.me + Z_STRIDE * i) % self.devices, i - 1).start()
        self.copy(k, self.me, self.y_peer, 3).start()
        self.copy(k, self.me, self.core_peer, 4).start()

    def pass_z(self, k):
        for i in range(1, Z_COUNT):
            origin = (self.me + Z_STRIDE * i) % self.devices
            self.copy(k, origin, self.y_peer, 0).wait_recv()
            self.copy(k, origin, self.y_peer, 4 + i).start()
            self.copy(k, origin, self.core_peer, 7 + i).start()

    def pass_y(self, k):
        for i in range(Z_COUNT):
            origin = (self.y_peer + Z_STRIDE * i) % self.devices
            self.copy(k, origin, self.y_peer, 0).wait_recv()
            self.copy(k, origin, self.core_peer, 11 + i).start()

    def arrive(self, k):
        def one(i, carry):
            origin = (self.core_peer + 2 * i) % self.devices
            self.copy(k, origin, self.y_peer, 0).wait_recv()
            return carry

        lax.fori_loop(0, self.devices // 2, one, 0)

    def finish(self):
        def one(i, carry):
            for k in range(CHUNKS):
                self.copy(k, self.me, self.y_peer, i).wait_send()
            return carry

        lax.fori_loop(0, self.devices - 1, one, 0)

    def run(self, work):
        self.own(1)
        self.pass_z(0)
        for k in range(CHUNKS):
            if k + 2 < CHUNKS:
                self.own(k + 2)
            if k + 1 < CHUNKS:
                self.pass_z(k + 1)
            self.pass_y(k)
            if k > 0:
                self.arrive(k - 1)
                work(k - 1)
        self.arrive(CHUNKS - 1)
        work(CHUNKS - 1)


class Exchange:
    def __init__(self, devices, me, outgoing, incoming, send_sem, recv_sem):
        self.devices, self.me, self.outgoing, self.incoming = devices, me, outgoing, incoming
        self.send_sem, self.recv_sem = send_sem, recv_sem

    def start(self, device):
        remote(
            self.outgoing.at[device],
            self.incoming.at[self.me],
            self.send_sem.at[device],
            self.recv_sem.at[self.me],
            device,
        ).start()

    def start_all(self):
        def one(i, carry):
            self.start((self.me + i) % self.devices)
            return carry

        lax.fori_loop(1, self.devices, one, 0)

    def arrive(self):
        self.incoming[self.me] = self.outgoing[self.me]

        def one(i, carry):
            device = (self.me + i) % self.devices
            remote(
                self.outgoing.at[device],
                self.incoming.at[device],
                self.send_sem.at[device],
                self.recv_sem.at[device],
                device,
            ).wait_recv()
            return carry

        lax.fori_loop(1, self.devices, one, 0)

    def finish(self):
        def one(i, carry):
            device = (self.me + i) % self.devices
            remote(
                self.outgoing.at[device],
                self.incoming.at[device],
                self.send_sem.at[device],
                self.recv_sem.at[device],
                device,
            ).wait_send()
            return carry

        lax.fori_loop(1, self.devices, one, 0)


TRANSPOSED = (((1,), (1,)), ((), ()))


def project_kernel(
    devices,
    hidden_ref,
    gain_ref,
    index_ref,
    table_ref,
    query_weight_ref,
    kv_weight_ref,
    down_ref,
    query_up_ref,
    kv_up_ref,
    q_out,
    kv_out,
    place_out,
    select_out,
    blocks,
    owner_blocks,
    wq,
    wr,
    up_q,
    up_kv,
    acc_q,
    acc_r,
    delta_send,
    delta_recv,
    rows_send,
    rows_recv,
    gather_send,
    gather_recv,
    owner_send,
    owner_recv,
    delta_ssem,
    delta_rsem,
    rows_ssem,
    rows_rsem,
    load_sem,
):
    me = lax.axis_index("replica")
    rows, width = hidden_ref.shape
    chunk = width // CHUNKS
    total = devices * rows
    capacity = 2 * rows
    columns = wq.shape[1]
    rank = up_q.shape[0]
    adapters = table_ref.shape[1]
    loads = [
        pltpu.make_async_copy(query_weight_ref, wq, load_sem.at[0]),
        pltpu.make_async_copy(kv_weight_ref, wr.at[pl.ds(0, 2)], load_sem.at[1]),
        pltpu.make_async_copy(down_ref.at[0, pl.ds(0, 3)], wr.at[pl.ds(2, 3)], load_sem.at[2]),
        pltpu.make_async_copy(query_up_ref.at[0], up_q, load_sem.at[3]),
        pltpu.make_async_copy(kv_up_ref.at[0], up_kv, load_sem.at[4]),
    ]
    for load in loads:
        load.start()
    values = hidden_ref[...].astype(jnp.float32)
    scaled = values * lax.rsqrt(jnp.mean(values * values, axis=-1, keepdims=True) + 1e-06)
    normed = (scaled * gain_ref[...]).astype(jnp.bfloat16)
    for k in range(CHUNKS):
        blocks[k, me] = normed[:, k * chunk : (k + 1) * chunk]
    picked = index_ref[...] == lax.broadcasted_iota(jnp.int32, (rows, adapters), 1)
    owner = jnp.sum(
        jnp.where(picked, table_ref[...].astype(jnp.float32), 0.0), axis=1, keepdims=True
    )
    owner_blocks[me] = jnp.broadcast_to(owner, (rows, 128)).astype(jnp.bfloat16)
    greet_all(devices, me)

    def owner_copy(device, origin):
        return remote(
            owner_blocks.at[me],
            owner_blocks.at[origin],
            owner_send.at[device],
            owner_recv.at[origin],
            device,
        )

    def send_owner(i, carry):
        owner_copy((me + i) % devices, me).start()
        return carry

    def wait_owner(i, carry):
        device = (me + i) % devices
        owner_copy(device, device).wait_recv()
        owner_copy(device, device).wait_send()
        return carry

    gather = Gather(devices, me, blocks, gather_send, gather_recv)

    def work(k):
        if k == 0:
            for load in loads:
                load.wait()
        x = blocks[k].reshape(total, chunk)
        part = pl.ds(k * chunk, chunk)
        q = jnp.dot(x, wq[part, :], preferred_element_type=jnp.float32)
        r = lax.dot_general(
            x,
            wr[:, :, part].reshape(5 * rank, chunk),
            TRANSPOSED,
            preferred_element_type=jnp.float32,
        )
        if k == 0:
            acc_q[...] = q
            acc_r[...] = r
        else:
            acc_q[...] += q
            acc_r[...] += r
        if k == 0:
            lax.fori_loop(1, devices, wait_owner, 0)
            owners = owner_blocks[...].reshape(total, 128).astype(jnp.float32)
            lane = lax.broadcasted_iota(jnp.int32, (total, 128), 1)
            member = jnp.where(owners.astype(jnp.int32) == lane, 1.0, 0.0)
            before = jnp.where(
                lax.broadcasted_iota(jnp.int32, (total, total), 0)
                >= lax.broadcasted_iota(jnp.int32, (total, total), 1),
                1.0,
                0.0,
            )
            running = jnp.dot(
                before.astype(jnp.bfloat16),
                member.astype(jnp.bfloat16),
                preferred_element_type=jnp.float32,
            )
            within = jnp.sum(running * member, axis=1, keepdims=True) - 1.0
            slot = (owners[:, :1] * capacity + within).astype(jnp.int32)
            slots = lax.broadcasted_iota(jnp.int32, (total, devices * capacity), 1)
            place_out[...] = jnp.where(slot == slots, 1.0, 0.0).astype(jnp.bfloat16)
            mine = jnp.where(slot == me * capacity + lane, 1.0, 0.0)
            select_out[...] = mine.T[:capacity].astype(jnp.bfloat16)

    gather.own(0)
    lax.fori_loop(1, devices, send_owner, 0)
    gather.run(work)

    factors = jnp.dot(
        select_out[...],
        acc_r[:, 2 * rank :].astype(jnp.bfloat16),
        preferred_element_type=jnp.float32,
    ).astype(jnp.bfloat16)
    kd = (
        adapter_scale
        * jnp.dot(factors[:, rank : 2 * rank], up_kv[0], preferred_element_type=jnp.float32)
    ).astype(jnp.bfloat16)
    vd = (
        adapter_scale
        * jnp.dot(factors[:, 2 * rank :], up_kv[1], preferred_element_type=jnp.float32)
    ).astype(jnp.bfloat16)
    for d in range(devices):
        pair = d // 2
        delta_send[d, :, columns : columns + 128] = kd[:, pair * 128 : (pair + 1) * 128]
        delta_send[d, :, columns + 128 :] = vd[:, pair * 128 : (pair + 1) * 128]
    deltas = Exchange(devices, me, delta_send, delta_recv, delta_ssem, delta_rsem)

    def update(device):
        begin = pl.multiple_of(device * columns, columns)
        delta_send[device, :, :columns] = (
            adapter_scale
            * jnp.dot(
                factors[:, :rank],
                up_q[:, pl.ds(begin, columns)],
                preferred_element_type=jnp.float32,
            )
        ).astype(jnp.bfloat16)

    def update_and_send(i, carry):
        device = (me + i) % devices
        update(device)
        deltas.start(device)
        return carry

    lax.fori_loop(1, devices, update_and_send, 0)
    update(me)
    deltas.arrive()
    added = jnp.dot(
        place_out[...],
        delta_recv[...].reshape(devices * capacity, columns + 256),
        preferred_element_type=jnp.float32,
    )
    rows_send[:, :, :columns] = (
        (acc_q[...] + added[:, :columns]).astype(jnp.bfloat16).reshape(devices, rows, columns)
    )
    even = me % 2 == 0
    k_added = jnp.where(even, added[:, columns : columns + 64], added[:, columns + 64 : columns + 128])
    v_added = jnp.where(even, added[:, columns + 128 : columns + 192], added[:, columns + 192 :])
    rows_send[:, :, columns:] = (
        (acc_r[:, : 2 * rank] + jnp.concatenate([k_added, v_added], axis=1))
        .astype(jnp.bfloat16)
        .reshape(devices, rows, 128)
    )
    exchange = Exchange(devices, me, rows_send, rows_recv, rows_ssem, rows_rsem)
    exchange.start_all()
    gather.finish()
    deltas.finish()
    exchange.arrive()
    for d in range(devices):
        q_out[:, d * columns : (d + 1) * columns] = rows_recv[d, :, :columns]
        kv_out[d] = rows_recv[d, :, columns:]
    exchange.finish()


def output_kernel(
    devices,
    attended_ref,
    place_ref,
    select_ref,
    output_weight_ref,
    down_ref,
    output_up_ref,
    out,
    blocks,
    wo,
    wd,
    up_o,
    acc_o,
    acc_f,
    delta_send,
    delta_recv,
    rows_send,
    rows_recv,
    gather_send,
    gather_recv,
    delta_ssem,
    delta_rsem,
    rows_ssem,
    rows_rsem,
    load_sem,
):
    me = lax.axis_index("replica")
    rows, width = attended_ref.shape
    chunk = width // CHUNKS
    total = devices * rows
    capacity = 2 * rows
    columns = wo.shape[1]
    loads = [
        pltpu.make_async_copy(output_weight_ref, wo, load_sem.at[0]),
        pltpu.make_async_copy(down_ref.at[0, 3], wd, load_sem.at[1]),
        pltpu.make_async_copy(output_up_ref.at[0], up_o, load_sem.at[2]),
    ]
    for load in loads:
        load.start()
    for k in range(CHUNKS):
        blocks[k, me] = attended_ref[:, k * chunk : (k + 1) * chunk]
    greet_all(devices, me)
    gather = Gather(devices, me, blocks, gather_send, gather_recv)

    def work(k):
        if k == 0:
            for load in loads:
                load.wait()
        x = blocks[k].reshape(total, chunk)
        part = pl.ds(k * chunk, chunk)
        o = jnp.dot(x, wo[part, :], preferred_element_type=jnp.float32)
        f = lax.dot_general(x, wd[:, part], TRANSPOSED, preferred_element_type=jnp.float32)
        if k == 0:
            acc_o[...] = o
            acc_f[...] = f
        else:
            acc_o[...] += o
            acc_f[...] += f

    gather.own(0)
    gather.run(work)
    factors = jnp.dot(
        select_ref[...], acc_f[...].astype(jnp.bfloat16), preferred_element_type=jnp.float32
    ).astype(jnp.bfloat16)
    deltas = Exchange(devices, me, delta_send, delta_recv, delta_ssem, delta_rsem)

    def update(device):
        begin = pl.multiple_of(device * columns, columns)
        delta_send[device] = (
            adapter_scale
            * jnp.dot(
                factors, up_o[:, pl.ds(begin, columns)], preferred_element_type=jnp.float32
            )
        ).astype(jnp.bfloat16)

    def update_and_send(i, carry):
        device = (me + i) % devices
        update(device)
        deltas.start(device)
        return carry

    lax.fori_loop(1, devices, update_and_send, 0)
    update(me)
    deltas.arrive()
    added = jnp.dot(
        place_ref[...],
        delta_recv[...].reshape(devices * capacity, columns),
        preferred_element_type=jnp.float32,
    )
    rows_send[...] = (acc_o[...] + added).astype(jnp.bfloat16).reshape(devices, rows, columns)
    exchange = Exchange(devices, me, rows_send, rows_recv, rows_ssem, rows_rsem)
    exchange.start_all()
    gather.finish()
    deltas.finish()
    exchange.arrive()
    for d in range(devices):
        out[:, d * columns : (d + 1) * columns] = rows_recv[d]
    exchange.finish()


def fused(
    hidden,
    input_norm_gain,
    row_adapter_index,
    adapter_slot_table,
    cache_length,
    rotated_key_cache,
    cached_value_table,
    query_weight,
    key_value_weight,
    output_weight,
    adapter_down_weight,
    query_up_weight,
    key_value_up_weight,
    output_up_weight,
):
    devices = lax.axis_size("replica")
    rows, width = hidden.shape
    total, capacity = devices * rows, 2 * rows
    columns = query_weight.shape[1]
    rank = query_up_weight.shape[1]
    bf16, f32 = jnp.bfloat16, jnp.float32
    in_vmem = pl.BlockSpec(memory_space=pltpu.VMEM)
    in_any = pl.BlockSpec(memory_space=pl.ANY)
    dma = pltpu.SemaphoreType.DMA
    q_rows, kv, place, select = pl.pallas_call(
        functools.partial(project_kernel, devices),
        out_shape=(
            jax.ShapeDtypeStruct((rows, width), bf16),
            jax.ShapeDtypeStruct((devices, rows, 128), bf16),
            jax.ShapeDtypeStruct((total, devices * capacity), bf16),
            jax.ShapeDtypeStruct((capacity, total), bf16),
        ),
        in_specs=[in_vmem] * 4 + [in_any] * 5,
        out_specs=(in_vmem,) * 4,
        scratch_shapes=[
            pltpu.VMEM((CHUNKS, devices, rows, width // CHUNKS), bf16),
            pltpu.VMEM((devices, rows, 128), bf16),
            pltpu.VMEM((width, columns), bf16),
            pltpu.VMEM((5, rank, width), bf16),
            pltpu.VMEM((rank, width), bf16),
            pltpu.VMEM(key_value_up_weight.shape[1:], bf16),
            pltpu.VMEM((total, columns), f32),
            pltpu.VMEM((total, 5 * rank), f32),
            pltpu.VMEM((devices, capacity, columns + 256), bf16),
            pltpu.VMEM((devices, capacity, columns + 256), bf16),
            pltpu.VMEM((devices, rows, columns + 128), bf16),
            pltpu.VMEM((devices, rows, columns + 128), bf16),
            dma((CHUNKS, devices)),
            dma((CHUNKS, devices)),
            dma((devices,)),
            dma((devices,)),
            dma((devices,)),
            dma((devices,)),
            dma((devices,)),
            dma((devices,)),
            dma((5,)),
        ],
        compiler_params=pltpu.CompilerParams(
            collective_id=0, has_side_effects=True, vmem_limit_bytes=48 * 2**20
        ),
        name="project",
    )(
        hidden,
        input_norm_gain.reshape(1, width),
        row_adapter_index,
        adapter_slot_table.reshape(1, -1),
        query_weight,
        key_value_weight,
        adapter_down_weight,
        query_up_weight,
        key_value_up_weight,
    )
    half = kv.shape[-1] // 2
    k_rows = kv[:, :, :half].transpose(1, 0, 2).reshape(rows, devices * half)
    v_rows = kv[:, :, half:].transpose(1, 0, 2).reshape(rows, devices * half)
    attended = attend(q_rows, k_rows, v_rows, cache_length, rotated_key_cache, cached_value_table)
    return pl.pallas_call(
        functools.partial(output_kernel, devices),
        out_shape=jax.ShapeDtypeStruct((rows, width), bf16),
        in_specs=[in_vmem] * 3 + [in_any] * 3,
        out_specs=in_vmem,
        scratch_shapes=[
            pltpu.VMEM((CHUNKS, devices, rows, width // CHUNKS), bf16),
            pltpu.VMEM((width, columns), bf16),
            pltpu.VMEM((rank, width), bf16),
            pltpu.VMEM((rank, width), bf16),
            pltpu.VMEM((total, columns), f32),
            pltpu.VMEM((total, rank), f32),
            pltpu.VMEM((devices, capacity, columns), bf16),
            pltpu.VMEM((devices, capacity, columns), bf16),
            pltpu.VMEM((devices, rows, columns), bf16),
            pltpu.VMEM((devices, rows, columns), bf16),
            dma((CHUNKS, devices)),
            dma((CHUNKS, devices)),
            dma((devices,)),
            dma((devices,)),
            dma((devices,)),
            dma((devices,)),
            dma((3,)),
        ],
        compiler_params=pltpu.CompilerParams(
            collective_id=1, has_side_effects=True, vmem_limit_bytes=48 * 2**20
        ),
        name="output",
    )(attended, place, select, output_weight, adapter_down_weight, output_up_weight)


def solution(mesh):
    in_specs = (
        P(("group", "replica"), None),
        P(),
        P(("group", "replica"), None),
        P(),
        P(("group", "replica")),
        P(("group", "replica"), None, None),
        P(("group", "replica"), None, None),
        P(None, "replica"),
        P(None, "replica", None),
        P(None, "replica"),
        P("replica", None, None, None),
        P("replica", None, None),
        P("replica", None, None, None),
        P("replica", None, None),
    )
    out_specs = P(("group", "replica"), None)
    body = fused if mesh.shape["replica"] == 16 else local
    return jax.shard_map(body, mesh=mesh, in_specs=in_specs, out_specs=out_specs, check_vma=False)
```

```python
import functools
import math

import jax
import jax.numpy as jnp
from jax import lax
from jax.experimental import pallas as pl
from jax.experimental.pallas import tpu as pltpu
from jax.sharding import PartitionSpec as P

HEADS = 64
KV_HEADS = 8
HD = 128
LENGTH = 96


adapter_scale = 0.5


def rms_norm(hidden, input_norm_gain):
    values = hidden.astype(jnp.float32)
    scaled = values * lax.rsqrt(jnp.mean(values * values, axis=-1, keepdims=True) + 1e-06)
    return (scaled * input_norm_gain).astype(jnp.bfloat16)


def rotate(values, position):
    half_width = HD // 2
    inv_freq = 1000000.0 ** (-(jnp.arange(half_width, dtype=jnp.float32) * 2.0 / HD))
    angles = position.astype(jnp.float32)[:, None, None] * inv_freq[None, None, :]
    cosine = jnp.concatenate([jnp.cos(angles), jnp.cos(angles)], axis=-1)
    sine_part = jnp.concatenate([jnp.sin(angles), jnp.sin(angles)], axis=-1)
    rotated = jnp.concatenate([-values[..., half_width:], values[..., :half_width]], axis=-1)
    return values * cosine + rotated * sine_part


def attend(queries, new_keys, new_values, cache_length, rotated_key_cache, cached_value_table):
    row_count = queries.shape[0]
    groups = HEADS // KV_HEADS
    scale_factor = 1.0 / math.sqrt(HD)
    heads_q = rotate(
        queries.astype(jnp.float32).reshape(row_count, HEADS, HD), cache_length
    ).astype(jnp.bfloat16)
    heads_k = rotate(
        new_keys.astype(jnp.float32).reshape(row_count, KV_HEADS, HD), cache_length
    ).astype(jnp.bfloat16)
    grouped_q = heads_q.reshape(row_count, KV_HEADS, groups, HD)
    cached_k = rotated_key_cache.reshape(row_count, LENGTH, KV_HEADS, HD)
    cached_v = cached_value_table.reshape(row_count, LENGTH, KV_HEADS, HD)
    scores = (
        jnp.einsum("rgjd,rtgd->rgjt", grouped_q, cached_k, preferred_element_type=jnp.float32)
        * scale_factor
    )
    own_score = (
        jnp.einsum("rgjd,rgd->rgj", grouped_q, heads_k, preferred_element_type=jnp.float32)
        * scale_factor
    )
    visible = (jnp.arange(LENGTH)[None, :] < cache_length[:, None])[:, None, None, :]
    masked = jnp.where(visible, scores, -1e30)
    largest = jnp.maximum(jnp.max(masked, axis=-1), own_score)
    weights = jnp.where(visible, jnp.exp(masked - largest[..., None]), 0.0)
    own_weight = jnp.exp(own_score - largest)
    denominator = jnp.sum(weights, axis=-1) + own_weight
    chances = (weights / denominator[..., None]).astype(jnp.bfloat16)
    own_chance = (own_weight / denominator).astype(jnp.bfloat16)
    mixed_values = jnp.einsum(
        "rgjt,rtgd->rgjd", chances, cached_v, preferred_element_type=jnp.float32
    )
    mixed_values = mixed_values + own_chance.astype(jnp.float32)[..., None] * new_values.astype(
        jnp.float32
    ).reshape(row_count, KV_HEADS, 1, HD)
    return mixed_values.reshape(row_count, HEADS * HD).astype(jnp.bfloat16)


def local(
    hidden,
    input_norm_gain,
    row_adapter_index,
    adapter_slot_table,
    cache_length,
    rotated_key_cache,
    cached_value_table,
    query_weight,
    key_value_weight,
    output_weight,
    adapter_down_weight,
    query_up_weight,
    key_value_up_weight,
    output_up_weight,
):
    devices = lax.axis_size("replica")
    myself = lax.axis_index("replica")
    local_rows = hidden.shape[0]
    capacity = 2 * local_rows
    adapters = adapter_slot_table.shape[0]
    normalized_input = rms_norm(hidden, input_norm_gain)
    picked = (row_adapter_index == jnp.arange(adapters)[None, :]).astype(jnp.int32)
    owner_devices = jnp.sum(picked * adapter_slot_table[None, :], axis=1)
    all_normed, all_owners = (
        lax.all_gather(normalized_input, "replica", axis=0, tiled=True),
        lax.all_gather(owner_devices, "replica", axis=0, tiled=True),
    )
    member = (all_owners[:, None] == jnp.arange(devices)[None, :]).astype(jnp.int32)
    running = jnp.cumsum(member, axis=0)
    position = all_owners * capacity + jnp.sum(running * member, axis=1) - 1
    my_slots = myself * capacity + jnp.arange(capacity)
    select = (position[None, :] == my_slots[:, None]).astype(jnp.bfloat16)
    my_rows = jnp.dot(select, all_normed, preferred_element_type=jnp.float32).astype(jnp.bfloat16)
    down_weight_maps = adapter_down_weight[0]
    factor_list = jnp.einsum(
        "cd,prd->cpr", my_rows, down_weight_maps[:3], preferred_element_type=jnp.float32
    ).astype(jnp.bfloat16)
    query_update = (
        adapter_scale
        * jnp.dot(factor_list[:, 0], query_up_weight[0], preferred_element_type=jnp.float32)
    ).astype(jnp.bfloat16)
    key_update = (
        adapter_scale
        * jnp.dot(factor_list[:, 1], key_value_up_weight[0, 0], preferred_element_type=jnp.float32)
    ).astype(jnp.bfloat16)
    value_update = (
        adapter_scale
        * jnp.dot(factor_list[:, 2], key_value_up_weight[0, 1], preferred_element_type=jnp.float32)
    ).astype(jnp.bfloat16)
    slot_q, slot_k, slot_v = (
        lax.all_to_all(query_update, "replica", split_axis=1, concat_axis=0, tiled=True),
        lax.all_to_all(key_update, "replica", split_axis=1, concat_axis=0, tiled=True),
        lax.all_to_all(value_update, "replica", split_axis=1, concat_axis=0, tiled=True),
    )
    contract = (((1,), (1,)), ((), ()))
    queries = jnp.dot(all_normed, query_weight, preferred_element_type=jnp.float32) + jnp.take(
        slot_q, position, axis=0
    ).astype(jnp.float32)
    key_new = lax.dot_general(
        all_normed, key_value_weight[0], contract, preferred_element_type=jnp.float32
    ) + jnp.take(slot_k, position, axis=0).astype(jnp.float32)
    value_new = lax.dot_general(
        all_normed, key_value_weight[1], contract, preferred_element_type=jnp.float32
    ) + jnp.take(slot_v, position, axis=0).astype(jnp.float32)
    q_rows, k_rows, v_rows = (
        lax.all_to_all(
            queries.astype(jnp.bfloat16), "replica", split_axis=0, concat_axis=1, tiled=True
        ),
        lax.all_to_all(
            key_new.astype(jnp.bfloat16), "replica", split_axis=0, concat_axis=1, tiled=True
        ),
        lax.all_to_all(
            value_new.astype(jnp.bfloat16), "replica", split_axis=0, concat_axis=1, tiled=True
        ),
    )
    attention_result = attend(
        q_rows, k_rows, v_rows, cache_length, rotated_key_cache, cached_value_table
    )
    attended_all = lax.all_gather(attention_result, "replica", axis=0, tiled=True)
    my_attended = jnp.dot(select, attended_all, preferred_element_type=jnp.float32).astype(
        jnp.bfloat16
    )
    output_factor = lax.dot_general(
        my_attended, down_weight_maps[3], contract, preferred_element_type=jnp.float32
    ).astype(jnp.bfloat16)
    output_update = adapter_scale * jnp.dot(
        output_factor, output_up_weight[0], preferred_element_type=jnp.float32
    )
    delta_cols = lax.all_to_all(
        output_update.astype(jnp.bfloat16), "replica", split_axis=1, concat_axis=0, tiled=True
    ).astype(output_update.dtype)
    partial_cols = jnp.dot(
        attended_all, output_weight, preferred_element_type=jnp.float32
    ) + jnp.take(delta_cols, position, axis=0)
    return lax.all_to_all(
        partial_cols.astype(jnp.bfloat16), "replica", split_axis=0, concat_axis=1, tiled=True
    )


CHUNKS = 4
Z_STRIDE = 4
Z_COUNT = 4


def remote(source, target, send_sem, recv_sem, device):
    return pltpu.make_async_remote_copy(
        src_ref=source,
        dst_ref=target,
        send_sem=send_sem,
        recv_sem=recv_sem,
        device_id={"replica": device},
        device_id_type=pl.DeviceIdType.MESH,
    )


def greet_all(devices, me):
    barrier = pltpu.get_barrier_semaphore()

    def greet(i, carry):
        pl.semaphore_signal(
            barrier,
            inc=1,
            device_id={"replica": (me + i) % devices},
            device_id_type=pl.DeviceIdType.MESH,
        )
        return carry

    lax.fori_loop(1, devices, greet, 0)
    pl.semaphore_wait(barrier, devices - 1)


class Gather:
    def __init__(self, devices, me, blocks, send_sem, recv_sem):
        self.devices, self.me, self.blocks = devices, me, blocks
        self.send_sem, self.recv_sem = send_sem, recv_sem
        self.y_peer = me + 2 - 4 * ((me // 2) % 2)
        self.core_peer = me + 1 - 2 * (me % 2)

    def copy(self, k, origin, device, number):
        block = self.blocks.at[k, origin]
        return remote(
            block, block, self.send_sem.at[k, number], self.recv_sem.at[k, origin], device
        )

    def own(self, k):
        for i in range(1, Z_COUNT):
            self.copy(k, self.me, (self.me + Z_STRIDE * i) % self.devices, i - 1).start()
        self.copy(k, self.me, self.y_peer, 3).start()
        self.copy(k, self.me, self.core_peer, 4).start()

    def pass_z(self, k):
        for i in range(1, Z_COUNT):
            origin = (self.me + Z_STRIDE * i) % self.devices
            self.copy(k, origin, self.y_peer, 0).wait_recv()
            self.copy(k, origin, self.y_peer, 4 + i).start()
            self.copy(k, origin, self.core_peer, 7 + i).start()

    def pass_y(self, k):
        for i in range(Z_COUNT):
            origin = (self.y_peer + Z_STRIDE * i) % self.devices
            self.copy(k, origin, self.y_peer, 0).wait_recv()
            self.copy(k, origin, self.core_peer, 11 + i).start()

    def arrive(self, k):
        def one(i, carry):
            origin = (self.core_peer + 2 * i) % self.devices
            self.copy(k, origin, self.y_peer, 0).wait_recv()
            return carry

        lax.fori_loop(0, self.devices // 2, one, 0)

    def finish(self):
        def one(i, carry):
            for k in range(CHUNKS):
                self.copy(k, self.me, self.y_peer, i).wait_send()
            return carry

        lax.fori_loop(0, self.devices - 1, one, 0)

    def run(self, work):
        self.own(1)
        self.pass_z(0)
        for k in range(CHUNKS):
            if k + 2 < CHUNKS:
                self.own(k + 2)
            if k + 1 < CHUNKS:
                self.pass_z(k + 1)
            self.pass_y(k)
            if k > 0:
                self.arrive(k - 1)
                work(k - 1)
        self.arrive(CHUNKS - 1)
        work(CHUNKS - 1)


class Exchange:
    def __init__(self, devices, me, outgoing, incoming, send_sem, recv_sem):
        self.devices, self.me, self.outgoing, self.incoming = devices, me, outgoing, incoming
        self.send_sem, self.recv_sem = send_sem, recv_sem

    def start(self, device):
        remote(
            self.outgoing.at[device],
            self.incoming.at[self.me],
            self.send_sem.at[device],
            self.recv_sem.at[self.me],
            device,
        ).start()

    def start_all(self):
        def one(i, carry):
            self.start((self.me + i) % self.devices)
            return carry

        lax.fori_loop(1, self.devices, one, 0)

    def arrive(self):
        self.incoming[self.me] = self.outgoing[self.me]

        def one(i, carry):
            device = (self.me + i) % self.devices
            remote(
                self.outgoing.at[device],
                self.incoming.at[device],
                self.send_sem.at[device],
                self.recv_sem.at[device],
                device,
            ).wait_recv()
            return carry

        lax.fori_loop(1, self.devices, one, 0)

    def finish(self):
        def one(i, carry):
            device = (self.me + i) % self.devices
            remote(
                self.outgoing.at[device],
                self.incoming.at[device],
                self.send_sem.at[device],
                self.recv_sem.at[device],
                device,
            ).wait_send()
            return carry

        lax.fori_loop(1, self.devices, one, 0)


TRANSPOSED = (((1,), (1,)), ((), ()))


def project_kernel(
    devices,
    hidden_ref,
    gain_ref,
    index_ref,
    table_ref,
    query_weight_ref,
    kv_weight_ref,
    down_ref,
    query_up_ref,
    kv_up_ref,
    q_out,
    kv_out,
    place_out,
    select_out,
    blocks,
    owner_blocks,
    wq,
    wr,
    up_q,
    up_kv,
    acc_q,
    acc_r,
    delta_send,
    delta_recv,
    rows_send,
    rows_recv,
    gather_send,
    gather_recv,
    owner_send,
    owner_recv,
    delta_ssem,
    delta_rsem,
    rows_ssem,
    rows_rsem,
    load_sem,
):
    me = lax.axis_index("replica")
    rows, width = hidden_ref.shape
    chunk = width // CHUNKS
    total = devices * rows
    capacity = 2 * rows
    columns = wq.shape[1]
    rank = up_q.shape[0]
    adapters = table_ref.shape[1]
    loads = [
        pltpu.make_async_copy(query_weight_ref, wq, load_sem.at[0]),
        pltpu.make_async_copy(kv_weight_ref, wr.at[pl.ds(0, 2)], load_sem.at[1]),
        pltpu.make_async_copy(down_ref.at[0, pl.ds(0, 3)], wr.at[pl.ds(2, 3)], load_sem.at[2]),
        pltpu.make_async_copy(query_up_ref.at[0], up_q, load_sem.at[3]),
        pltpu.make_async_copy(kv_up_ref.at[0], up_kv, load_sem.at[4]),
    ]
    for load in loads:
        load.start()
    values = hidden_ref[...].astype(jnp.float32)
    scaled = values * lax.rsqrt(jnp.mean(values * values, axis=-1, keepdims=True) + 1e-06)
    normed = (scaled * gain_ref[...]).astype(jnp.bfloat16)
    for k in range(CHUNKS):
        blocks[k, me] = normed[:, k * chunk : (k + 1) * chunk]
    picked = index_ref[...] == lax.broadcasted_iota(jnp.int32, (rows, adapters), 1)
    owner = jnp.sum(
        jnp.where(picked, table_ref[...].astype(jnp.float32), 0.0), axis=1, keepdims=True
    )
    owner_blocks[me] = jnp.broadcast_to(owner, (rows, 128)).astype(jnp.bfloat16)
    greet_all(devices, me)

    def owner_copy(device, origin):
        return remote(
            owner_blocks.at[me],
            owner_blocks.at[origin],
            owner_send.at[device],
            owner_recv.at[origin],
            device,
        )

    def send_owner(i, carry):
        owner_copy((me + i) % devices, me).start()
        return carry

    def wait_owner(i, carry):
        device = (me + i) % devices
        owner_copy(device, device).wait_recv()
        owner_copy(device, device).wait_send()
        return carry

    gather = Gather(devices, me, blocks, gather_send, gather_recv)

    def work(k):
        if k == 0:
            for load in loads:
                load.wait()
        x = blocks[k].reshape(total, chunk)
        part = pl.ds(k * chunk, chunk)
        q = jnp.dot(x, wq[part, :], preferred_element_type=jnp.float32)
        r = lax.dot_general(
            x,
            wr[:, :, part].reshape(5 * rank, chunk),
            TRANSPOSED,
            preferred_element_type=jnp.float32,
        )
        if k == 0:
            acc_q[...] = q
            acc_r[...] = r
        else:
            acc_q[...] += q
            acc_r[...] += r
        if k == 0:
            lax.fori_loop(1, devices, wait_owner, 0)
            owners = owner_blocks[...].reshape(total, 128).astype(jnp.float32)
            lane = lax.broadcasted_iota(jnp.int32, (total, 128), 1)
            member = jnp.where(owners.astype(jnp.int32) == lane, 1.0, 0.0)
            before = jnp.where(
                lax.broadcasted_iota(jnp.int32, (total, total), 0)
                >= lax.broadcasted_iota(jnp.int32, (total, total), 1),
                1.0,
                0.0,
            )
            running = jnp.dot(
                before.astype(jnp.bfloat16),
                member.astype(jnp.bfloat16),
                preferred_element_type=jnp.float32,
            )
            within = jnp.sum(running * member, axis=1, keepdims=True) - 1.0
            slot = (owners[:, :1] * capacity + within).astype(jnp.int32)
            slots = lax.broadcasted_iota(jnp.int32, (total, devices * capacity), 1)
            place_out[...] = jnp.where(slot == slots, 1.0, 0.0).astype(jnp.bfloat16)
            mine = jnp.where(slot == me * capacity + lane, 1.0, 0.0)
            select_out[...] = mine.T[:capacity].astype(jnp.bfloat16)

    gather.own(0)
    lax.fori_loop(1, devices, send_owner, 0)
    gather.run(work)

    factors = jnp.dot(
        select_out[...],
        acc_r[:, 2 * rank :].astype(jnp.bfloat16),
        preferred_element_type=jnp.float32,
    ).astype(jnp.bfloat16)
    kd = (
        adapter_scale
        * jnp.dot(factors[:, rank : 2 * rank], up_kv[0], preferred_element_type=jnp.float32)
    ).astype(jnp.bfloat16)
    vd = (
        adapter_scale
        * jnp.dot(factors[:, 2 * rank :], up_kv[1], preferred_element_type=jnp.float32)
    ).astype(jnp.bfloat16)
    for d in range(devices):
        delta_send[d, :, columns:] = jnp.concatenate(
            [kd[:, d * 64 : (d + 1) * 64], vd[:, d * 64 : (d + 1) * 64]], axis=1
        )
    deltas = Exchange(devices, me, delta_send, delta_recv, delta_ssem, delta_rsem)

    def update(device):
        begin = pl.multiple_of(device * columns, columns)
        delta_send[device, :, :columns] = (
            adapter_scale
            * jnp.dot(
                factors[:, :rank],
                up_q[:, pl.ds(begin, columns)],
                preferred_element_type=jnp.float32,
            )
        ).astype(jnp.bfloat16)

    def update_and_send(i, carry):
        device = (me + i) % devices
        update(device)
        deltas.start(device)
        return carry

    lax.fori_loop(1, devices, update_and_send, 0)
    update(me)
    deltas.arrive()
    added = jnp.dot(
        place_out[...],
        delta_recv[...].reshape(devices * capacity, columns + 128),
        preferred_element_type=jnp.float32,
    )
    rows_send[:, :, :columns] = (
        (acc_q[...] + added[:, :columns]).astype(jnp.bfloat16).reshape(devices, rows, columns)
    )
    rows_send[:, :, columns:] = (
        (acc_r[:, : 2 * rank] + added[:, columns:])
        .astype(jnp.bfloat16)
        .reshape(devices, rows, 128)
    )
    exchange = Exchange(devices, me, rows_send, rows_recv, rows_ssem, rows_rsem)
    exchange.start_all()
    gather.finish()
    deltas.finish()
    exchange.arrive()
    for d in range(devices):
        q_out[:, d * columns : (d + 1) * columns] = rows_recv[d, :, :columns]
        kv_out[d] = rows_recv[d, :, columns:]
    exchange.finish()


def output_kernel(
    devices,
    attended_ref,
    place_ref,
    select_ref,
    output_weight_ref,
    down_ref,
    output_up_ref,
    out,
    blocks,
    wo,
    wd,
    up_o,
    acc_o,
    acc_f,
    delta_send,
    delta_recv,
    rows_send,
    rows_recv,
    gather_send,
    gather_recv,
    delta_ssem,
    delta_rsem,
    rows_ssem,
    rows_rsem,
    load_sem,
):
    me = lax.axis_index("replica")
    rows, width = attended_ref.shape
    chunk = width // CHUNKS
    total = devices * rows
    capacity = 2 * rows
    columns = wo.shape[1]
    loads = [
        pltpu.make_async_copy(output_weight_ref, wo, load_sem.at[0]),
        pltpu.make_async_copy(down_ref.at[0, 3], wd, load_sem.at[1]),
        pltpu.make_async_copy(output_up_ref.at[0], up_o, load_sem.at[2]),
    ]
    for load in loads:
        load.start()
    for k in range(CHUNKS):
        blocks[k, me] = attended_ref[:, k * chunk : (k + 1) * chunk]
    greet_all(devices, me)
    gather = Gather(devices, me, blocks, gather_send, gather_recv)

    def work(k):
        if k == 0:
            for load in loads:
                load.wait()
        x = blocks[k].reshape(total, chunk)
        part = pl.ds(k * chunk, chunk)
        o = jnp.dot(x, wo[part, :], preferred_element_type=jnp.float32)
        f = lax.dot_general(x, wd[:, part], TRANSPOSED, preferred_element_type=jnp.float32)
        if k == 0:
            acc_o[...] = o
            acc_f[...] = f
        else:
            acc_o[...] += o
            acc_f[...] += f

    gather.own(0)
    gather.run(work)
    factors = jnp.dot(
        select_ref[...], acc_f[...].astype(jnp.bfloat16), preferred_element_type=jnp.float32
    ).astype(jnp.bfloat16)
    deltas = Exchange(devices, me, delta_send, delta_recv, delta_ssem, delta_rsem)

    def update(device):
        begin = pl.multiple_of(device * columns, columns)
        delta_send[device] = (
            adapter_scale
            * jnp.dot(
                factors, up_o[:, pl.ds(begin, columns)], preferred_element_type=jnp.float32
            )
        ).astype(jnp.bfloat16)

    def update_and_send(i, carry):
        device = (me + i) % devices
        update(device)
        deltas.start(device)
        return carry

    lax.fori_loop(1, devices, update_and_send, 0)
    update(me)
    deltas.arrive()
    added = jnp.dot(
        place_ref[...],
        delta_recv[...].reshape(devices * capacity, columns),
        preferred_element_type=jnp.float32,
    )
    rows_send[...] = (acc_o[...] + added).astype(jnp.bfloat16).reshape(devices, rows, columns)
    exchange = Exchange(devices, me, rows_send, rows_recv, rows_ssem, rows_rsem)
    exchange.start_all()
    gather.finish()
    deltas.finish()
    exchange.arrive()
    for d in range(devices):
        out[:, d * columns : (d + 1) * columns] = rows_recv[d]
    exchange.finish()


def fused(
    hidden,
    input_norm_gain,
    row_adapter_index,
    adapter_slot_table,
    cache_length,
    rotated_key_cache,
    cached_value_table,
    query_weight,
    key_value_weight,
    output_weight,
    adapter_down_weight,
    query_up_weight,
    key_value_up_weight,
    output_up_weight,
):
    devices = lax.axis_size("replica")
    rows, width = hidden.shape
    total, capacity = devices * rows, 2 * rows
    columns = query_weight.shape[1]
    rank = query_up_weight.shape[1]
    bf16, f32 = jnp.bfloat16, jnp.float32
    in_vmem = pl.BlockSpec(memory_space=pltpu.VMEM)
    in_any = pl.BlockSpec(memory_space=pl.ANY)
    dma = pltpu.SemaphoreType.DMA
    q_rows, kv, place, select = pl.pallas_call(
        functools.partial(project_kernel, devices),
        out_shape=(
            jax.ShapeDtypeStruct((rows, width), bf16),
            jax.ShapeDtypeStruct((devices, rows, 128), bf16),
            jax.ShapeDtypeStruct((total, devices * capacity), bf16),
            jax.ShapeDtypeStruct((capacity, total), bf16),
        ),
        in_specs=[in_vmem] * 4 + [in_any] * 5,
        out_specs=(in_vmem,) * 4,
        scratch_shapes=[
            pltpu.VMEM((CHUNKS, devices, rows, width // CHUNKS), bf16),
            pltpu.VMEM((devices, rows, 128), bf16),
            pltpu.VMEM((width, columns), bf16),
            pltpu.VMEM((5, rank, width), bf16),
            pltpu.VMEM((rank, width), bf16),
            pltpu.VMEM(key_value_up_weight.shape[1:], bf16),
            pltpu.VMEM((total, columns), f32),
            pltpu.VMEM((total, 5 * rank), f32),
            pltpu.VMEM((devices, capacity, columns + 128), bf16),
            pltpu.VMEM((devices, capacity, columns + 128), bf16),
            pltpu.VMEM((devices, rows, columns + 128), bf16),
            pltpu.VMEM((devices, rows, columns + 128), bf16),
            dma((CHUNKS, devices)),
            dma((CHUNKS, devices)),
            dma((devices,)),
            dma((devices,)),
            dma((devices,)),
            dma((devices,)),
            dma((devices,)),
            dma((devices,)),
            dma((5,)),
        ],
        compiler_params=pltpu.CompilerParams(
            collective_id=0, has_side_effects=True, vmem_limit_bytes=60 * 2**20
        ),
        name="project",
    )(
        hidden,
        input_norm_gain.reshape(1, width),
        row_adapter_index,
        adapter_slot_table.reshape(1, -1),
        query_weight,
        key_value_weight,
        adapter_down_weight,
        query_up_weight,
        key_value_up_weight,
    )
    half = kv.shape[-1] // 2
    k_rows = kv[:, :, :half].transpose(1, 0, 2).reshape(rows, devices * half)
    v_rows = kv[:, :, half:].transpose(1, 0, 2).reshape(rows, devices * half)
    attended = attend(q_rows, k_rows, v_rows, cache_length, rotated_key_cache, cached_value_table)
    return pl.pallas_call(
        functools.partial(output_kernel, devices),
        out_shape=jax.ShapeDtypeStruct((rows, width), bf16),
        in_specs=[in_vmem] * 3 + [in_any] * 3,
        out_specs=in_vmem,
        scratch_shapes=[
            pltpu.VMEM((CHUNKS, devices, rows, width // CHUNKS), bf16),
            pltpu.VMEM((width, columns), bf16),
            pltpu.VMEM((rank, width), bf16),
            pltpu.VMEM((rank, width), bf16),
            pltpu.VMEM((total, columns), f32),
            pltpu.VMEM((total, rank), f32),
            pltpu.VMEM((devices, capacity, columns), bf16),
            pltpu.VMEM((devices, capacity, columns), bf16),
            pltpu.VMEM((devices, rows, columns), bf16),
            pltpu.VMEM((devices, rows, columns), bf16),
            dma((CHUNKS, devices)),
            dma((CHUNKS, devices)),
            dma((devices,)),
            dma((devices,)),
            dma((devices,)),
            dma((devices,)),
            dma((3,)),
        ],
        compiler_params=pltpu.CompilerParams(
            collective_id=1, has_side_effects=True, vmem_limit_bytes=60 * 2**20
        ),
        name="output",
    )(attended, place, select, output_weight, adapter_down_weight, output_up_weight)


def solution(mesh):
    in_specs = (
        P(("group", "replica"), None),
        P(),
        P(("group", "replica"), None),
        P(),
        P(("group", "replica")),
        P(("group", "replica"), None, None),
        P(("group", "replica"), None, None),
        P(None, "replica"),
        P(None, "replica", None),
        P(None, "replica"),
        P("replica", None, None, None),
        P("replica", None, None),
        P("replica", None, None, None),
        P("replica", None, None),
    )
    out_specs = P(("group", "replica"), None)
    body = fused if mesh.shape["replica"] == 16 else local
    return jax.shard_map(body, mesh=mesh, in_specs=in_specs, out_specs=out_specs, check_vma=False)
```

```python
import functools
import math

import jax
import jax.numpy as jnp
from jax import lax
from jax.experimental import pallas as pl
from jax.experimental.pallas import tpu as pltpu
from jax.sharding import PartitionSpec as P

HEADS = 64
KV_HEADS = 8
HD = 128
LENGTH = 96


adapter_scale = 0.5


def rms_norm(hidden, input_norm_gain):
    values = hidden.astype(jnp.float32)
    scaled = values * lax.rsqrt(jnp.mean(values * values, axis=-1, keepdims=True) + 1e-06)
    return (scaled * input_norm_gain).astype(jnp.bfloat16)


def rotate(values, position):
    half_width = HD // 2
    inv_freq = 1000000.0 ** (-(jnp.arange(half_width, dtype=jnp.float32) * 2.0 / HD))
    angles = position.astype(jnp.float32)[:, None, None] * inv_freq[None, None, :]
    cosine = jnp.concatenate([jnp.cos(angles), jnp.cos(angles)], axis=-1)
    sine_part = jnp.concatenate([jnp.sin(angles), jnp.sin(angles)], axis=-1)
    rotated = jnp.concatenate([-values[..., half_width:], values[..., :half_width]], axis=-1)
    return values * cosine + rotated * sine_part


def attend(queries, new_keys, new_values, cache_length, rotated_key_cache, cached_value_table):
    row_count = queries.shape[0]
    groups = HEADS // KV_HEADS
    scale_factor = 1.0 / math.sqrt(HD)
    heads_q = rotate(
        queries.astype(jnp.float32).reshape(row_count, HEADS, HD), cache_length
    ).astype(jnp.bfloat16)
    heads_k = rotate(
        new_keys.astype(jnp.float32).reshape(row_count, KV_HEADS, HD), cache_length
    ).astype(jnp.bfloat16)
    grouped_q = heads_q.reshape(row_count, KV_HEADS, groups, HD)
    cached_k = rotated_key_cache.reshape(row_count, LENGTH, KV_HEADS, HD)
    cached_v = cached_value_table.reshape(row_count, LENGTH, KV_HEADS, HD)
    scores = (
        jnp.einsum("rgjd,rtgd->rgjt", grouped_q, cached_k, preferred_element_type=jnp.float32)
        * scale_factor
    )
    own_score = (
        jnp.einsum("rgjd,rgd->rgj", grouped_q, heads_k, preferred_element_type=jnp.float32)
        * scale_factor
    )
    visible = (jnp.arange(LENGTH)[None, :] < cache_length[:, None])[:, None, None, :]
    masked = jnp.where(visible, scores, -1e30)
    largest = jnp.maximum(jnp.max(masked, axis=-1), own_score)
    weights = jnp.where(visible, jnp.exp(masked - largest[..., None]), 0.0)
    own_weight = jnp.exp(own_score - largest)
    denominator = jnp.sum(weights, axis=-1) + own_weight
    chances = (weights / denominator[..., None]).astype(jnp.bfloat16)
    own_chance = (own_weight / denominator).astype(jnp.bfloat16)
    mixed_values = jnp.einsum(
        "rgjt,rtgd->rgjd", chances, cached_v, preferred_element_type=jnp.float32
    )
    mixed_values = mixed_values + own_chance.astype(jnp.float32)[..., None] * new_values.astype(
        jnp.float32
    ).reshape(row_count, KV_HEADS, 1, HD)
    return mixed_values.reshape(row_count, HEADS * HD).astype(jnp.bfloat16)


def local(
    hidden,
    input_norm_gain,
    row_adapter_index,
    adapter_slot_table,
    cache_length,
    rotated_key_cache,
    cached_value_table,
    query_weight,
    key_value_weight,
    output_weight,
    adapter_down_weight,
    query_up_weight,
    key_value_up_weight,
    output_up_weight,
):
    devices = lax.axis_size("replica")
    myself = lax.axis_index("replica")
    local_rows = hidden.shape[0]
    capacity = 2 * local_rows
    adapters = adapter_slot_table.shape[0]
    normalized_input = rms_norm(hidden, input_norm_gain)
    picked = (row_adapter_index == jnp.arange(adapters)[None, :]).astype(jnp.int32)
    owner_devices = jnp.sum(picked * adapter_slot_table[None, :], axis=1)
    all_normed, all_owners = (
        lax.all_gather(normalized_input, "replica", axis=0, tiled=True),
        lax.all_gather(owner_devices, "replica", axis=0, tiled=True),
    )
    member = (all_owners[:, None] == jnp.arange(devices)[None, :]).astype(jnp.int32)
    running = jnp.cumsum(member, axis=0)
    position = all_owners * capacity + jnp.sum(running * member, axis=1) - 1
    my_slots = myself * capacity + jnp.arange(capacity)
    select = (position[None, :] == my_slots[:, None]).astype(jnp.bfloat16)
    my_rows = jnp.dot(select, all_normed, preferred_element_type=jnp.float32).astype(jnp.bfloat16)
    down_weight_maps = adapter_down_weight[0]
    factor_list = jnp.einsum(
        "cd,prd->cpr", my_rows, down_weight_maps[:3], preferred_element_type=jnp.float32
    ).astype(jnp.bfloat16)
    query_update = (
        adapter_scale
        * jnp.dot(factor_list[:, 0], query_up_weight[0], preferred_element_type=jnp.float32)
    ).astype(jnp.bfloat16)
    key_update = (
        adapter_scale
        * jnp.dot(factor_list[:, 1], key_value_up_weight[0, 0], preferred_element_type=jnp.float32)
    ).astype(jnp.bfloat16)
    value_update = (
        adapter_scale
        * jnp.dot(factor_list[:, 2], key_value_up_weight[0, 1], preferred_element_type=jnp.float32)
    ).astype(jnp.bfloat16)
    slot_q, slot_k, slot_v = (
        lax.all_to_all(query_update, "replica", split_axis=1, concat_axis=0, tiled=True),
        lax.all_to_all(key_update, "replica", split_axis=1, concat_axis=0, tiled=True),
        lax.all_to_all(value_update, "replica", split_axis=1, concat_axis=0, tiled=True),
    )
    contract = (((1,), (1,)), ((), ()))
    queries = jnp.dot(all_normed, query_weight, preferred_element_type=jnp.float32) + jnp.take(
        slot_q, position, axis=0
    ).astype(jnp.float32)
    key_new = lax.dot_general(
        all_normed, key_value_weight[0], contract, preferred_element_type=jnp.float32
    ) + jnp.take(slot_k, position, axis=0).astype(jnp.float32)
    value_new = lax.dot_general(
        all_normed, key_value_weight[1], contract, preferred_element_type=jnp.float32
    ) + jnp.take(slot_v, position, axis=0).astype(jnp.float32)
    q_rows, k_rows, v_rows = (
        lax.all_to_all(
            queries.astype(jnp.bfloat16), "replica", split_axis=0, concat_axis=1, tiled=True
        ),
        lax.all_to_all(
            key_new.astype(jnp.bfloat16), "replica", split_axis=0, concat_axis=1, tiled=True
        ),
        lax.all_to_all(
            value_new.astype(jnp.bfloat16), "replica", split_axis=0, concat_axis=1, tiled=True
        ),
    )
    attention_result = attend(
        q_rows, k_rows, v_rows, cache_length, rotated_key_cache, cached_value_table
    )
    attended_all = lax.all_gather(attention_result, "replica", axis=0, tiled=True)
    my_attended = jnp.dot(select, attended_all, preferred_element_type=jnp.float32).astype(
        jnp.bfloat16
    )
    output_factor = lax.dot_general(
        my_attended, down_weight_maps[3], contract, preferred_element_type=jnp.float32
    ).astype(jnp.bfloat16)
    output_update = adapter_scale * jnp.dot(
        output_factor, output_up_weight[0], preferred_element_type=jnp.float32
    )
    delta_cols = lax.all_to_all(
        output_update.astype(jnp.bfloat16), "replica", split_axis=1, concat_axis=0, tiled=True
    ).astype(output_update.dtype)
    partial_cols = jnp.dot(
        attended_all, output_weight, preferred_element_type=jnp.float32
    ) + jnp.take(delta_cols, position, axis=0)
    return lax.all_to_all(
        partial_cols.astype(jnp.bfloat16), "replica", split_axis=0, concat_axis=1, tiled=True
    )


CHUNKS = 4
Z_STRIDE = 4
Z_COUNT = 4


def remote(source, target, send_sem, recv_sem, device):
    return pltpu.make_async_remote_copy(
        src_ref=source,
        dst_ref=target,
        send_sem=send_sem,
        recv_sem=recv_sem,
        device_id={"replica": device},
        device_id_type=pl.DeviceIdType.MESH,
    )


def greet_all(devices, me):
    barrier = pltpu.get_barrier_semaphore()

    def greet(i, carry):
        pl.semaphore_signal(
            barrier,
            inc=1,
            device_id={"replica": (me + i) % devices},
            device_id_type=pl.DeviceIdType.MESH,
        )
        return carry

    lax.fori_loop(1, devices, greet, 0)


def await_all(devices):
    pl.semaphore_wait(pltpu.get_barrier_semaphore(), devices - 1)


class Gather:
    def __init__(self, devices, me, blocks, send_sem, recv_sem):
        self.devices, self.me, self.blocks = devices, me, blocks
        self.send_sem, self.recv_sem = send_sem, recv_sem
        self.y_peer = me + 2 - 4 * ((me // 2) % 2)
        self.core_peer = me + 1 - 2 * (me % 2)

    def copy(self, k, origin, device, number):
        block = self.blocks.at[k, origin]
        return remote(
            block, block, self.send_sem.at[k, number], self.recv_sem.at[k, origin], device
        )

    def own(self, k):
        for i in range(1, Z_COUNT):
            self.copy(k, self.me, (self.me + Z_STRIDE * i) % self.devices, i - 1).start()
        self.copy(k, self.me, self.y_peer, 3).start()
        self.copy(k, self.me, self.core_peer, 4).start()

    def pass_z(self, k):
        for i in range(1, Z_COUNT):
            origin = (self.me + Z_STRIDE * i) % self.devices
            self.copy(k, origin, self.y_peer, 0).wait_recv()
            self.copy(k, origin, self.y_peer, 4 + i).start()
            self.copy(k, origin, self.core_peer, 7 + i).start()

    def pass_y(self, k):
        for i in range(Z_COUNT):
            origin = (self.y_peer + Z_STRIDE * i) % self.devices
            self.copy(k, origin, self.y_peer, 0).wait_recv()
            self.copy(k, origin, self.core_peer, 11 + i).start()

    def arrive(self, k):
        def one(i, carry):
            origin = (self.core_peer + 2 * i) % self.devices
            self.copy(k, origin, self.y_peer, 0).wait_recv()
            return carry

        lax.fori_loop(0, self.devices // 2, one, 0)

    def finish(self):
        def one(i, carry):
            for k in range(CHUNKS):
                self.copy(k, self.me, self.y_peer, i).wait_send()
            return carry

        lax.fori_loop(0, self.devices - 1, one, 0)

    def run(self, work):
        self.own(1)
        self.pass_z(0)
        for k in range(CHUNKS):
            if k + 2 < CHUNKS:
                self.own(k + 2)
            if k + 1 < CHUNKS:
                self.pass_z(k + 1)
            self.pass_y(k)
            if k > 0:
                self.arrive(k - 1)
                work(k - 1)
        self.arrive(CHUNKS - 1)
        work(CHUNKS - 1)


class Exchange:
    def __init__(self, devices, me, outgoing, incoming, send_sem, recv_sem):
        self.devices, self.me, self.outgoing, self.incoming = devices, me, outgoing, incoming
        self.send_sem, self.recv_sem = send_sem, recv_sem

    def start(self, device):
        remote(
            self.outgoing.at[device],
            self.incoming.at[self.me],
            self.send_sem.at[device],
            self.recv_sem.at[self.me],
            device,
        ).start()

    def start_all(self):
        def one(i, carry):
            self.start((self.me + i) % self.devices)
            return carry

        lax.fori_loop(1, self.devices, one, 0)

    def arrive(self):
        self.incoming[self.me] = self.outgoing[self.me]

        def one(i, carry):
            device = (self.me + i) % self.devices
            remote(
                self.outgoing.at[device],
                self.incoming.at[device],
                self.send_sem.at[device],
                self.recv_sem.at[device],
                device,
            ).wait_recv()
            return carry

        lax.fori_loop(1, self.devices, one, 0)

    def finish(self):
        def one(i, carry):
            device = (self.me + i) % self.devices
            remote(
                self.outgoing.at[device],
                self.incoming.at[device],
                self.send_sem.at[device],
                self.recv_sem.at[device],
                device,
            ).wait_send()
            return carry

        lax.fori_loop(1, self.devices, one, 0)


TRANSPOSED = (((1,), (1,)), ((), ()))


def project_kernel(
    devices,
    hidden_ref,
    gain_ref,
    index_ref,
    table_ref,
    query_weight_ref,
    kv_weight_ref,
    down_ref,
    query_up_ref,
    kv_up_ref,
    q_out,
    k_out,
    v_out,
    place_out,
    select_out,
    blocks,
    owner_blocks,
    wq,
    wr,
    up_q,
    up_kv,
    acc_q,
    acc_r,
    delta_send,
    delta_recv,
    rows_send,
    rows_recv,
    gather_send,
    gather_recv,
    owner_send,
    owner_recv,
    delta_ssem,
    delta_rsem,
    rows_ssem,
    rows_rsem,
    load_sem,
):
    me = lax.axis_index("replica")
    rows, width = hidden_ref.shape
    chunk = width // CHUNKS
    total = devices * rows
    capacity = 2 * rows
    columns = wq.shape[1]
    rank = up_q.shape[0]
    loads = [
        pltpu.make_async_copy(query_weight_ref, wq, load_sem.at[0]),
        pltpu.make_async_copy(kv_weight_ref, wr.at[pl.ds(0, 2)], load_sem.at[1]),
        pltpu.make_async_copy(down_ref.at[0, pl.ds(0, 3)], wr.at[pl.ds(2, 3)], load_sem.at[2]),
        pltpu.make_async_copy(query_up_ref.at[0], up_q, load_sem.at[3]),
        pltpu.make_async_copy(kv_up_ref.at[0], up_kv, load_sem.at[4]),
    ]
    for load in loads:
        load.start()
    values = hidden_ref[...].astype(jnp.float32)
    scaled = values * lax.rsqrt(jnp.mean(values * values, axis=-1, keepdims=True) + 1e-06)
    normed = (scaled * gain_ref[...]).astype(jnp.bfloat16)
    for k in range(CHUNKS):
        blocks[k, me] = normed[:, k * chunk : (k + 1) * chunk]
    owner = jnp.zeros((rows, 128), jnp.int32)
    row = lax.broadcasted_iota(jnp.int32, (rows, 128), 0)
    for r in range(rows):
        owner = jnp.where(row == r, table_ref[index_ref[r]], owner)
    owner_blocks[me] = owner.astype(jnp.float32).astype(jnp.bfloat16)
    greet_all(devices, me)
    await_all(devices)

    def owner_copy(device, origin):
        return remote(
            owner_blocks.at[me],
            owner_blocks.at[origin],
            owner_send.at[device],
            owner_recv.at[origin],
            device,
        )

    def send_owner(i, carry):
        owner_copy((me + i) % devices, me).start()
        return carry

    def wait_owner(i, carry):
        device = (me + i) % devices
        owner_copy(device, device).wait_recv()
        owner_copy(device, device).wait_send()
        return carry

    gather = Gather(devices, me, blocks, gather_send, gather_recv)

    def work(k):
        if k == 0:
            for load in loads:
                load.wait()
        x = blocks[k].reshape(total, chunk)
        part = pl.ds(k * chunk, chunk)
        q = jnp.dot(x, wq[part, :], preferred_element_type=jnp.float32)
        r = lax.dot_general(
            x,
            wr[:, :, part].reshape(5 * rank, chunk),
            TRANSPOSED,
            preferred_element_type=jnp.float32,
        )
        if k == 0:
            acc_q[...] = q
            acc_r[...] = r
        else:
            acc_q[...] += q
            acc_r[...] += r
        if k == 0:
            lax.fori_loop(1, devices, wait_owner, 0)
            owners = owner_blocks[...].reshape(total, 128).astype(jnp.float32)
            lane = lax.broadcasted_iota(jnp.int32, (total, 128), 1)
            member = jnp.where(owners.astype(jnp.int32) == lane, 1.0, 0.0)
            before = jnp.where(
                lax.broadcasted_iota(jnp.int32, (total, total), 0)
                >= lax.broadcasted_iota(jnp.int32, (total, total), 1),
                1.0,
                0.0,
            )
            running = jnp.dot(
                before.astype(jnp.bfloat16),
                member.astype(jnp.bfloat16),
                preferred_element_type=jnp.float32,
            )
            within = jnp.sum(running * member, axis=1, keepdims=True) - 1.0
            slot = (owners[:, :1] * capacity + within).astype(jnp.int32)
            slots = lax.broadcasted_iota(jnp.int32, (total, devices * capacity), 1)
            place_out[...] = jnp.where(slot == slots, 1.0, 0.0).astype(jnp.bfloat16)
            mine = jnp.where(slot == me * capacity + lane, 1.0, 0.0)
            select_out[...] = mine.T[:capacity].astype(jnp.bfloat16)

    gather.own(0)
    lax.fori_loop(1, devices, send_owner, 0)
    gather.run(work)

    factors = jnp.dot(
        select_out[...],
        acc_r[:, 2 * rank :].astype(jnp.bfloat16),
        preferred_element_type=jnp.float32,
    ).astype(jnp.bfloat16)
    kd = (
        adapter_scale
        * jnp.dot(factors[:, rank : 2 * rank], up_kv[0], preferred_element_type=jnp.float32)
    ).astype(jnp.bfloat16)
    vd = (
        adapter_scale
        * jnp.dot(factors[:, 2 * rank :], up_kv[1], preferred_element_type=jnp.float32)
    ).astype(jnp.bfloat16)
    for d in range(devices):
        delta_send[d, :, columns:] = jnp.concatenate(
            [kd[:, d * 64 : (d + 1) * 64], vd[:, d * 64 : (d + 1) * 64]], axis=1
        )
    deltas = Exchange(devices, me, delta_send, delta_recv, delta_ssem, delta_rsem)

    def update(device):
        begin = pl.multiple_of(device * columns, columns)
        delta_send[device, :, :columns] = (
            adapter_scale
            * jnp.dot(
                factors[:, :rank],
                up_q[:, pl.ds(begin, columns)],
                preferred_element_type=jnp.float32,
            )
        ).astype(jnp.bfloat16)

    def update_and_send(i, carry):
        device = (me + i) % devices
        update(device)
        deltas.start(device)
        return carry

    lax.fori_loop(1, devices, update_and_send, 0)
    update(me)
    deltas.arrive()
    added = jnp.dot(
        place_out[...],
        delta_recv[...].reshape(devices * capacity, columns + 128),
        preferred_element_type=jnp.float32,
    )
    rows_send[:, :, :columns] = (
        (acc_q[...] + added[:, :columns]).astype(jnp.bfloat16).reshape(devices, rows, columns)
    )
    rows_send[:, :, columns:] = (
        (acc_r[:, : 2 * rank] + added[:, columns:])
        .astype(jnp.bfloat16)
        .reshape(devices, rows, 128)
    )
    exchange = Exchange(devices, me, rows_send, rows_recv, rows_ssem, rows_rsem)
    exchange.start_all()
    gather.finish()
    deltas.finish()
    exchange.arrive()
    for d in range(devices):
        for j in range(columns // HD):
            q_out[:, d * (columns // HD) + j, :] = rows_recv[d, :, j * HD : (j + 1) * HD].astype(
                jnp.float32
            )
    for g in range(KV_HEADS):
        first = rows_recv[2 * g, :, columns:].astype(jnp.float32)
        second = rows_recv[2 * g + 1, :, columns:].astype(jnp.float32)
        k_out[:, g, :] = jnp.concatenate([first[:, :64], second[:, :64]], axis=1)
        v_out[:, g, :] = jnp.concatenate([first[:, 64:], second[:, 64:]], axis=1)
    exchange.finish()


def attend_row(q, k_new, v_new, cosine, sine, visible, cached_k, cached_v):
    heads, size = q.shape
    groups = k_new.shape[0]
    per_group = heads // groups
    scale_factor = 1.0 / math.sqrt(size)

    def turn(x):
        x = x.astype(jnp.float32)
        turned = x * cosine + pltpu.roll(x, size // 2, 1) * sine
        return turned.astype(jnp.bfloat16).astype(jnp.float32)

    def spread(x):
        return jnp.broadcast_to(x[:, None, :], (groups, per_group, size)).reshape(heads, size)

    q_turned = turn(q)
    wide = (heads, groups * size)
    mine = (
        lax.broadcasted_iota(jnp.int32, wide, 0) // per_group
        == lax.broadcasted_iota(jnp.int32, wide, 1) // size
    )
    q_wide = jnp.where(mine, jnp.concatenate([q_turned] * groups, axis=1), 0.0)
    scores = scale_factor * lax.dot_general(
        q_wide.astype(jnp.bfloat16), cached_k, TRANSPOSED, preferred_element_type=jnp.float32
    )
    own_score = scale_factor * jnp.sum(
        q_turned * spread(turn(k_new)), axis=1, keepdims=True
    )
    masked = jnp.where(visible, scores, -1e30)
    largest = jnp.maximum(jnp.max(masked, axis=1, keepdims=True), own_score)
    weights = jnp.where(visible, jnp.exp(masked - largest), 0.0)
    own_weight = jnp.exp(own_score - largest)
    denominator = jnp.sum(weights, axis=1, keepdims=True) + own_weight
    chances = (weights / denominator).astype(jnp.bfloat16)
    own_chance = (own_weight / denominator).astype(jnp.bfloat16).astype(jnp.float32)
    mixed = jnp.dot(chances, cached_v, preferred_element_type=jnp.float32)
    mixed = jnp.concatenate(
        [
            mixed[g * per_group : (g + 1) * per_group, g * size : (g + 1) * size]
            for g in range(groups)
        ],
        axis=0,
    )
    return mixed + own_chance * spread(v_new.astype(jnp.float32))


def output_kernel(
    devices,
    q_ref,
    k_ref,
    v_ref,
    cosine_ref,
    sine_ref,
    length_ref,
    key_cache_ref,
    value_cache_ref,
    place_ref,
    select_ref,
    output_weight_ref,
    down_ref,
    output_up_ref,
    out,
    blocks,
    wo,
    wd,
    up_o,
    acc_o,
    acc_f,
    delta_send,
    delta_recv,
    rows_send,
    rows_recv,
    gather_send,
    gather_recv,
    delta_ssem,
    delta_rsem,
    rows_ssem,
    rows_rsem,
    load_sem,
    cached_k,
    cached_v,
    attended,
):
    me = lax.axis_index("replica")
    rows, heads, size = q_ref.shape
    width = heads * size
    greet_all(devices, me)
    cache_loads = [
        pltpu.make_async_copy(key_cache_ref, cached_k, load_sem.at[3]),
        pltpu.make_async_copy(value_cache_ref, cached_v, load_sem.at[4]),
    ]
    for load in cache_loads:
        load.start()
    chunk = width // CHUNKS
    total = devices * rows
    capacity = 2 * rows
    columns = wo.shape[1]
    loads = [
        pltpu.make_async_copy(output_weight_ref, wo, load_sem.at[0]),
        pltpu.make_async_copy(down_ref.at[0, 3], wd, load_sem.at[1]),
        pltpu.make_async_copy(output_up_ref.at[0], up_o, load_sem.at[2]),
    ]
    for load in loads:
        load.start()
    for load in cache_loads:
        load.wait()
    length = cached_k.shape[1]
    for r in range(rows):
        visible = (
            lax.broadcasted_iota(jnp.int32, (heads, length), 1) < length_ref[r]
        )
        attended[r * heads : (r + 1) * heads, :] = attend_row(
            q_ref[r],
            k_ref[r],
            v_ref[r],
            cosine_ref[r : r + 1, :],
            sine_ref[r : r + 1, :],
            visible,
            cached_k[r],
            cached_v[r],
        )
    chunk_heads = heads // CHUNKS
    for h in range(heads):
        place = h % chunk_heads * size
        blocks[h // chunk_heads, me, :, place : place + size] = attended[
            pl.ds(h, rows, stride=heads), :
        ].astype(jnp.bfloat16)
    await_all(devices)
    gather = Gather(devices, me, blocks, gather_send, gather_recv)

    def work(k):
        if k == 0:
            for load in loads:
                load.wait()
        x = blocks[k].reshape(total, chunk)
        part = pl.ds(k * chunk, chunk)
        o = jnp.dot(x, wo[part, :], preferred_element_type=jnp.float32)
        f = lax.dot_general(x, wd[:, part], TRANSPOSED, preferred_element_type=jnp.float32)
        if k == 0:
            acc_o[...] = o
            acc_f[...] = f
        else:
            acc_o[...] += o
            acc_f[...] += f

    gather.own(0)
    gather.run(work)
    factors = jnp.dot(
        select_ref[...], acc_f[...].astype(jnp.bfloat16), preferred_element_type=jnp.float32
    ).astype(jnp.bfloat16)
    deltas = Exchange(devices, me, delta_send, delta_recv, delta_ssem, delta_rsem)

    def update(device):
        begin = pl.multiple_of(device * columns, columns)
        delta_send[device] = (
            adapter_scale
            * jnp.dot(
                factors, up_o[:, pl.ds(begin, columns)], preferred_element_type=jnp.float32
            )
        ).astype(jnp.bfloat16)

    def update_and_send(i, carry):
        device = (me + i) % devices
        update(device)
        deltas.start(device)
        return carry

    lax.fori_loop(1, devices, update_and_send, 0)
    update(me)
    deltas.arrive()
    added = jnp.dot(
        place_ref[...],
        delta_recv[...].reshape(devices * capacity, columns),
        preferred_element_type=jnp.float32,
    )
    rows_send[...] = (acc_o[...] + added).astype(jnp.bfloat16).reshape(devices, rows, columns)
    exchange = Exchange(devices, me, rows_send, rows_recv, rows_ssem, rows_rsem)
    exchange.start_all()
    gather.finish()
    deltas.finish()
    exchange.arrive()
    for d in range(devices):
        out[:, d * columns : (d + 1) * columns] = rows_recv[d]
    exchange.finish()


def fused(
    hidden,
    input_norm_gain,
    row_adapter_index,
    adapter_slot_table,
    cache_length,
    rotated_key_cache,
    cached_value_table,
    query_weight,
    key_value_weight,
    output_weight,
    adapter_down_weight,
    query_up_weight,
    key_value_up_weight,
    output_up_weight,
):
    devices = lax.axis_size("replica")
    rows, width = hidden.shape
    total, capacity = devices * rows, 2 * rows
    columns = query_weight.shape[1]
    rank = query_up_weight.shape[1]
    bf16, f32 = jnp.bfloat16, jnp.float32
    in_vmem = pl.BlockSpec(memory_space=pltpu.VMEM)
    in_smem = pl.BlockSpec(memory_space=pltpu.SMEM)
    in_any = pl.BlockSpec(memory_space=pl.ANY)
    dma = pltpu.SemaphoreType.DMA
    q_rows, k_rows, v_rows, place, select = pl.pallas_call(
        functools.partial(project_kernel, devices),
        out_shape=(
            jax.ShapeDtypeStruct((rows, HEADS, HD), f32),
            jax.ShapeDtypeStruct((rows, KV_HEADS, HD), f32),
            jax.ShapeDtypeStruct((rows, KV_HEADS, HD), f32),
            jax.ShapeDtypeStruct((total, devices * capacity), bf16),
            jax.ShapeDtypeStruct((capacity, total), bf16),
        ),
        in_specs=[in_vmem] * 2 + [in_smem] * 2 + [in_any] * 5,
        out_specs=(in_vmem,) * 5,
        scratch_shapes=[
            pltpu.VMEM((CHUNKS, devices, rows, width // CHUNKS), bf16),
            pltpu.VMEM((devices, rows, 128), bf16),
            pltpu.VMEM((width, columns), bf16),
            pltpu.VMEM((5, rank, width), bf16),
            pltpu.VMEM((rank, width), bf16),
            pltpu.VMEM(key_value_up_weight.shape[1:], bf16),
            pltpu.VMEM((total, columns), f32),
            pltpu.VMEM((total, 5 * rank), f32),
            pltpu.VMEM((devices, capacity, columns + 128), bf16),
            pltpu.VMEM((devices, capacity, columns + 128), bf16),
            pltpu.VMEM((devices, rows, columns + 128), bf16),
            pltpu.VMEM((devices, rows, columns + 128), bf16),
            dma((CHUNKS, devices)),
            dma((CHUNKS, devices)),
            dma((devices,)),
            dma((devices,)),
            dma((devices,)),
            dma((devices,)),
            dma((devices,)),
            dma((devices,)),
            dma((5,)),
        ],
        compiler_params=pltpu.CompilerParams(
            collective_id=0, has_side_effects=True, vmem_limit_bytes=60 * 2**20
        ),
        name="project",
    )(
        hidden,
        input_norm_gain.reshape(1, width),
        row_adapter_index.reshape(rows),
        adapter_slot_table,
        query_weight,
        key_value_weight,
        adapter_down_weight,
        query_up_weight,
        key_value_up_weight,
    )
    inv_freq = 1000000.0 ** (-(jnp.arange(HD // 2, dtype=f32) * 2.0 / HD))
    angles = cache_length.astype(f32)[:, None] * inv_freq[None, :]
    cosine = jnp.concatenate([jnp.cos(angles), jnp.cos(angles)], axis=-1)
    sine = jnp.concatenate([-jnp.sin(angles), jnp.sin(angles)], axis=-1)
    return pl.pallas_call(
        functools.partial(output_kernel, devices),
        out_shape=jax.ShapeDtypeStruct((rows, width), bf16),
        in_specs=[in_vmem] * 5 + [in_smem] + [in_any] * 2 + [in_vmem] * 2 + [in_any] * 3,
        out_specs=in_vmem,
        scratch_shapes=[
            pltpu.VMEM((CHUNKS, devices, rows, width // CHUNKS), bf16),
            pltpu.VMEM((width, columns), bf16),
            pltpu.VMEM((rank, width), bf16),
            pltpu.VMEM((rank, width), bf16),
            pltpu.VMEM((total, columns), f32),
            pltpu.VMEM((total, rank), f32),
            pltpu.VMEM((devices, capacity, columns), bf16),
            pltpu.VMEM((devices, capacity, columns), bf16),
            pltpu.VMEM((devices, rows, columns), bf16),
            pltpu.VMEM((devices, rows, columns), bf16),
            dma((CHUNKS, devices)),
            dma((CHUNKS, devices)),
            dma((devices,)),
            dma((devices,)),
            dma((devices,)),
            dma((devices,)),
            dma((5,)),
            pltpu.VMEM(rotated_key_cache.shape, bf16),
            pltpu.VMEM(cached_value_table.shape, bf16),
            pltpu.VMEM((rows * HEADS, HD), f32),
        ],
        compiler_params=pltpu.CompilerParams(
            collective_id=1, has_side_effects=True, vmem_limit_bytes=60 * 2**20
        ),
        name="output",
    )(
        q_rows,
        k_rows,
        v_rows,
        cosine,
        sine,
        cache_length,
        rotated_key_cache,
        cached_value_table,
        place,
        select,
        output_weight,
        adapter_down_weight,
        output_up_weight,
    )


def solution(mesh):
    in_specs = (
        P(("group", "replica"), None),
        P(),
        P(("group", "replica"), None),
        P(),
        P(("group", "replica")),
        P(("group", "replica"), None, None),
        P(("group", "replica"), None, None),
        P(None, "replica"),
        P(None, "replica", None),
        P(None, "replica"),
        P("replica", None, None, None),
        P("replica", None, None),
        P("replica", None, None, None),
        P("replica", None, None),
    )
    out_specs = P(("group", "replica"), None)
    body = fused if mesh.shape["replica"] == 16 else local
    return jax.shard_map(body, mesh=mesh, in_specs=in_specs, out_specs=out_specs, check_vma=False)
```

```python
import functools
import math

import jax
import jax.numpy as jnp
from jax import lax
from jax.experimental import pallas as pl
from jax.experimental.pallas import tpu as pltpu
from jax.sharding import PartitionSpec as P

HEADS = 64
KV_HEADS = 8
HD = 128
LENGTH = 96


adapter_scale = 0.5


def rms_norm(hidden, input_norm_gain):
    values = hidden.astype(jnp.float32)
    scaled = values * lax.rsqrt(jnp.mean(values * values, axis=-1, keepdims=True) + 1e-06)
    return (scaled * input_norm_gain).astype(jnp.bfloat16)


def rotate(values, position):
    half_width = HD // 2
    inv_freq = 1000000.0 ** (-(jnp.arange(half_width, dtype=jnp.float32) * 2.0 / HD))
    angles = position.astype(jnp.float32)[:, None, None] * inv_freq[None, None, :]
    cosine = jnp.concatenate([jnp.cos(angles), jnp.cos(angles)], axis=-1)
    sine_part = jnp.concatenate([jnp.sin(angles), jnp.sin(angles)], axis=-1)
    rotated = jnp.concatenate([-values[..., half_width:], values[..., :half_width]], axis=-1)
    return values * cosine + rotated * sine_part


def attend(queries, new_keys, new_values, cache_length, rotated_key_cache, cached_value_table):
    row_count = queries.shape[0]
    groups = HEADS // KV_HEADS
    scale_factor = 1.0 / math.sqrt(HD)
    heads_q = rotate(
        queries.astype(jnp.float32).reshape(row_count, HEADS, HD), cache_length
    ).astype(jnp.bfloat16)
    heads_k = rotate(
        new_keys.astype(jnp.float32).reshape(row_count, KV_HEADS, HD), cache_length
    ).astype(jnp.bfloat16)
    grouped_q = heads_q.reshape(row_count, KV_HEADS, groups, HD)
    cached_k = rotated_key_cache.reshape(row_count, LENGTH, KV_HEADS, HD)
    cached_v = cached_value_table.reshape(row_count, LENGTH, KV_HEADS, HD)
    scores = (
        jnp.einsum("rgjd,rtgd->rgjt", grouped_q, cached_k, preferred_element_type=jnp.float32)
        * scale_factor
    )
    own_score = (
        jnp.einsum("rgjd,rgd->rgj", grouped_q, heads_k, preferred_element_type=jnp.float32)
        * scale_factor
    )
    visible = (jnp.arange(LENGTH)[None, :] < cache_length[:, None])[:, None, None, :]
    masked = jnp.where(visible, scores, -1e30)
    largest = jnp.maximum(jnp.max(masked, axis=-1), own_score)
    weights = jnp.where(visible, jnp.exp(masked - largest[..., None]), 0.0)
    own_weight = jnp.exp(own_score - largest)
    denominator = jnp.sum(weights, axis=-1) + own_weight
    chances = (weights / denominator[..., None]).astype(jnp.bfloat16)
    own_chance = (own_weight / denominator).astype(jnp.bfloat16)
    mixed_values = jnp.einsum(
        "rgjt,rtgd->rgjd", chances, cached_v, preferred_element_type=jnp.float32
    )
    mixed_values = mixed_values + own_chance.astype(jnp.float32)[..., None] * new_values.astype(
        jnp.float32
    ).reshape(row_count, KV_HEADS, 1, HD)
    return mixed_values.reshape(row_count, HEADS * HD).astype(jnp.bfloat16)


def local(
    hidden,
    input_norm_gain,
    row_adapter_index,
    adapter_slot_table,
    cache_length,
    rotated_key_cache,
    cached_value_table,
    query_weight,
    key_value_weight,
    output_weight,
    adapter_down_weight,
    query_up_weight,
    key_value_up_weight,
    output_up_weight,
):
    devices = lax.axis_size("replica")
    myself = lax.axis_index("replica")
    local_rows = hidden.shape[0]
    capacity = 2 * local_rows
    adapters = adapter_slot_table.shape[0]
    normalized_input = rms_norm(hidden, input_norm_gain)
    picked = (row_adapter_index == jnp.arange(adapters)[None, :]).astype(jnp.int32)
    owner_devices = jnp.sum(picked * adapter_slot_table[None, :], axis=1)
    all_normed, all_owners = (
        lax.all_gather(normalized_input, "replica", axis=0, tiled=True),
        lax.all_gather(owner_devices, "replica", axis=0, tiled=True),
    )
    member = (all_owners[:, None] == jnp.arange(devices)[None, :]).astype(jnp.int32)
    running = jnp.cumsum(member, axis=0)
    position = all_owners * capacity + jnp.sum(running * member, axis=1) - 1
    my_slots = myself * capacity + jnp.arange(capacity)
    select = (position[None, :] == my_slots[:, None]).astype(jnp.bfloat16)
    my_rows = jnp.dot(select, all_normed, preferred_element_type=jnp.float32).astype(jnp.bfloat16)
    down_weight_maps = adapter_down_weight[0]
    factor_list = jnp.einsum(
        "cd,prd->cpr", my_rows, down_weight_maps[:3], preferred_element_type=jnp.float32
    ).astype(jnp.bfloat16)
    query_update = (
        adapter_scale
        * jnp.dot(factor_list[:, 0], query_up_weight[0], preferred_element_type=jnp.float32)
    ).astype(jnp.bfloat16)
    key_update = (
        adapter_scale
        * jnp.dot(factor_list[:, 1], key_value_up_weight[0, 0], preferred_element_type=jnp.float32)
    ).astype(jnp.bfloat16)
    value_update = (
        adapter_scale
        * jnp.dot(factor_list[:, 2], key_value_up_weight[0, 1], preferred_element_type=jnp.float32)
    ).astype(jnp.bfloat16)
    slot_q, slot_k, slot_v = (
        lax.all_to_all(query_update, "replica", split_axis=1, concat_axis=0, tiled=True),
        lax.all_to_all(key_update, "replica", split_axis=1, concat_axis=0, tiled=True),
        lax.all_to_all(value_update, "replica", split_axis=1, concat_axis=0, tiled=True),
    )
    contract = (((1,), (1,)), ((), ()))
    queries = jnp.dot(all_normed, query_weight, preferred_element_type=jnp.float32) + jnp.take(
        slot_q, position, axis=0
    ).astype(jnp.float32)
    key_new = lax.dot_general(
        all_normed, key_value_weight[0], contract, preferred_element_type=jnp.float32
    ) + jnp.take(slot_k, position, axis=0).astype(jnp.float32)
    value_new = lax.dot_general(
        all_normed, key_value_weight[1], contract, preferred_element_type=jnp.float32
    ) + jnp.take(slot_v, position, axis=0).astype(jnp.float32)
    q_rows, k_rows, v_rows = (
        lax.all_to_all(
            queries.astype(jnp.bfloat16), "replica", split_axis=0, concat_axis=1, tiled=True
        ),
        lax.all_to_all(
            key_new.astype(jnp.bfloat16), "replica", split_axis=0, concat_axis=1, tiled=True
        ),
        lax.all_to_all(
            value_new.astype(jnp.bfloat16), "replica", split_axis=0, concat_axis=1, tiled=True
        ),
    )
    attention_result = attend(
        q_rows, k_rows, v_rows, cache_length, rotated_key_cache, cached_value_table
    )
    attended_all = lax.all_gather(attention_result, "replica", axis=0, tiled=True)
    my_attended = jnp.dot(select, attended_all, preferred_element_type=jnp.float32).astype(
        jnp.bfloat16
    )
    output_factor = lax.dot_general(
        my_attended, down_weight_maps[3], contract, preferred_element_type=jnp.float32
    ).astype(jnp.bfloat16)
    output_update = adapter_scale * jnp.dot(
        output_factor, output_up_weight[0], preferred_element_type=jnp.float32
    )
    delta_cols = lax.all_to_all(
        output_update.astype(jnp.bfloat16), "replica", split_axis=1, concat_axis=0, tiled=True
    ).astype(output_update.dtype)
    partial_cols = jnp.dot(
        attended_all, output_weight, preferred_element_type=jnp.float32
    ) + jnp.take(delta_cols, position, axis=0)
    return lax.all_to_all(
        partial_cols.astype(jnp.bfloat16), "replica", split_axis=0, concat_axis=1, tiled=True
    )


CHUNKS = 4
Z_STRIDE = 4
Z_COUNT = 4


def remote(source, target, send_sem, recv_sem, device):
    return pltpu.make_async_remote_copy(
        src_ref=source,
        dst_ref=target,
        send_sem=send_sem,
        recv_sem=recv_sem,
        device_id={"replica": device},
        device_id_type=pl.DeviceIdType.MESH,
    )


def greet_all(devices, me):
    barrier = pltpu.get_barrier_semaphore()

    def greet(i, carry):
        pl.semaphore_signal(
            barrier,
            inc=1,
            device_id={"replica": (me + i) % devices},
            device_id_type=pl.DeviceIdType.MESH,
        )
        return carry

    lax.fori_loop(1, devices, greet, 0)


def await_all(devices):
    pl.semaphore_wait(pltpu.get_barrier_semaphore(), devices - 1)


class Gather:
    def __init__(self, devices, me, blocks, send_sem, recv_sem):
        self.devices, self.me, self.blocks = devices, me, blocks
        self.send_sem, self.recv_sem = send_sem, recv_sem
        self.y_peer = me + 2 - 4 * ((me // 2) % 2)
        self.core_peer = me + 1 - 2 * (me % 2)

    def copy(self, k, origin, device, number):
        block = self.blocks.at[k, origin]
        return remote(
            block, block, self.send_sem.at[k, number], self.recv_sem.at[k, origin], device
        )

    def own(self, k):
        for i in range(1, Z_COUNT):
            self.copy(k, self.me, (self.me + Z_STRIDE * i) % self.devices, i - 1).start()
        self.copy(k, self.me, self.y_peer, 3).start()
        self.copy(k, self.me, self.core_peer, 4).start()

    def pass_z(self, k):
        for i in range(1, Z_COUNT):
            origin = (self.me + Z_STRIDE * i) % self.devices
            self.copy(k, origin, self.y_peer, 0).wait_recv()
            self.copy(k, origin, self.y_peer, 4 + i).start()
            self.copy(k, origin, self.core_peer, 7 + i).start()

    def pass_y(self, k):
        for i in range(Z_COUNT):
            origin = (self.y_peer + Z_STRIDE * i) % self.devices
            self.copy(k, origin, self.y_peer, 0).wait_recv()
            self.copy(k, origin, self.core_peer, 11 + i).start()

    def arrive(self, k):
        def one(i, carry):
            origin = (self.core_peer + 2 * i) % self.devices
            self.copy(k, origin, self.y_peer, 0).wait_recv()
            return carry

        lax.fori_loop(0, self.devices // 2, one, 0)

    def finish(self):
        def one(i, carry):
            for k in range(CHUNKS):
                self.copy(k, self.me, self.y_peer, i).wait_send()
            return carry

        lax.fori_loop(0, self.devices - 1, one, 0)

    def run(self, work):
        self.own(1)
        self.pass_z(0)
        for k in range(CHUNKS):
            if k + 2 < CHUNKS:
                self.own(k + 2)
            if k + 1 < CHUNKS:
                self.pass_z(k + 1)
            self.pass_y(k)
            if k > 0:
                self.arrive(k - 1)
                work(k - 1)
        self.arrive(CHUNKS - 1)
        work(CHUNKS - 1)


class Exchange:
    def __init__(self, devices, me, outgoing, incoming, send_sem, recv_sem):
        self.devices, self.me, self.outgoing, self.incoming = devices, me, outgoing, incoming
        self.send_sem, self.recv_sem = send_sem, recv_sem

    def start(self, device):
        remote(
            self.outgoing.at[device],
            self.incoming.at[self.me],
            self.send_sem.at[device],
            self.recv_sem.at[self.me],
            device,
        ).start()

    def start_all(self):
        def one(i, carry):
            self.start((self.me + i) % self.devices)
            return carry

        lax.fori_loop(1, self.devices, one, 0)

    def arrive(self):
        self.incoming[self.me] = self.outgoing[self.me]

        def one(i, carry):
            device = (self.me + i) % self.devices
            remote(
                self.outgoing.at[device],
                self.incoming.at[device],
                self.send_sem.at[device],
                self.recv_sem.at[device],
                device,
            ).wait_recv()
            return carry

        lax.fori_loop(1, self.devices, one, 0)

    def finish(self):
        def one(i, carry):
            device = (self.me + i) % self.devices
            remote(
                self.outgoing.at[device],
                self.incoming.at[device],
                self.send_sem.at[device],
                self.recv_sem.at[device],
                device,
            ).wait_send()
            return carry

        lax.fori_loop(1, self.devices, one, 0)


TRANSPOSED = (((1,), (1,)), ((), ()))


def project_kernel(
    devices,
    hidden_ref,
    gain_ref,
    index_ref,
    table_ref,
    query_weight_ref,
    kv_weight_ref,
    down_ref,
    query_up_ref,
    kv_up_ref,
    q_out,
    k_out,
    v_out,
    place_out,
    select_out,
    blocks,
    owner_blocks,
    wq,
    wr,
    up_q,
    up_kv,
    acc_q,
    acc_r,
    delta_send,
    delta_recv,
    rows_send,
    rows_recv,
    gather_send,
    gather_recv,
    owner_send,
    owner_recv,
    delta_ssem,
    delta_rsem,
    rows_ssem,
    rows_rsem,
    load_sem,
):
    me = lax.axis_index("replica")
    rows, width = hidden_ref.shape
    greet_all(devices, me)
    chunk = width // CHUNKS
    total = devices * rows
    capacity = 2 * rows
    columns = wq.shape[1]
    rank = up_q.shape[0]
    loads = [
        pltpu.make_async_copy(query_weight_ref, wq, load_sem.at[0]),
        pltpu.make_async_copy(kv_weight_ref, wr.at[pl.ds(0, 2)], load_sem.at[1]),
        pltpu.make_async_copy(down_ref.at[0, pl.ds(0, 3)], wr.at[pl.ds(2, 3)], load_sem.at[2]),
        pltpu.make_async_copy(query_up_ref.at[0], up_q, load_sem.at[3]),
        pltpu.make_async_copy(kv_up_ref.at[0], up_kv, load_sem.at[4]),
    ]
    for load in loads:
        load.start()
    values = hidden_ref[...].astype(jnp.float32)
    scaled = values * lax.rsqrt(jnp.mean(values * values, axis=-1, keepdims=True) + 1e-06)
    normed = (scaled * gain_ref[...]).astype(jnp.bfloat16)
    for k in range(CHUNKS):
        blocks[k, me] = normed[:, k * chunk : (k + 1) * chunk]
    owner = jnp.zeros((rows, 128), jnp.int32)
    row = lax.broadcasted_iota(jnp.int32, (rows, 128), 0)
    for r in range(rows):
        owner = jnp.where(row == r, table_ref[index_ref[r]], owner)
    owner_blocks[me] = owner.astype(jnp.float32).astype(jnp.bfloat16)
    await_all(devices)

    def owner_copy(device, origin):
        return remote(
            owner_blocks.at[me],
            owner_blocks.at[origin],
            owner_send.at[device],
            owner_recv.at[origin],
            device,
        )

    def send_owner(i, carry):
        owner_copy((me + i) % devices, me).start()
        return carry

    def wait_owner(i, carry):
        device = (me + i) % devices
        owner_copy(device, device).wait_recv()
        owner_copy(device, device).wait_send()
        return carry

    gather = Gather(devices, me, blocks, gather_send, gather_recv)

    def work(k):
        if k == 0:
            for load in loads:
                load.wait()
        x = blocks[k].reshape(total, chunk)
        part = pl.ds(k * chunk, chunk)
        q = jnp.dot(x, wq[part, :], preferred_element_type=jnp.float32)
        r = lax.dot_general(
            x,
            wr[:, :, part].reshape(5 * rank, chunk),
            TRANSPOSED,
            preferred_element_type=jnp.float32,
        )
        if k == 0:
            acc_q[...] = q
            acc_r[...] = r
        else:
            acc_q[...] += q
            acc_r[...] += r
        if k == 0:
            lax.fori_loop(1, devices, wait_owner, 0)
            owners = owner_blocks[...].reshape(total, 128).astype(jnp.float32)
            lane = lax.broadcasted_iota(jnp.int32, (total, 128), 1)
            member = jnp.where(owners.astype(jnp.int32) == lane, 1.0, 0.0)
            before = jnp.where(
                lax.broadcasted_iota(jnp.int32, (total, total), 0)
                >= lax.broadcasted_iota(jnp.int32, (total, total), 1),
                1.0,
                0.0,
            )
            running = jnp.dot(
                before.astype(jnp.bfloat16),
                member.astype(jnp.bfloat16),
                preferred_element_type=jnp.float32,
            )
            within = jnp.sum(running * member, axis=1, keepdims=True) - 1.0
            slot = (owners[:, :1] * capacity + within).astype(jnp.int32)
            slots = lax.broadcasted_iota(jnp.int32, (total, devices * capacity), 1)
            place_out[...] = jnp.where(slot == slots, 1.0, 0.0).astype(jnp.bfloat16)
            mine = jnp.where(slot == me * capacity + lane, 1.0, 0.0)
            select_out[...] = mine.T[:capacity].astype(jnp.bfloat16)

    gather.own(0)
    lax.fori_loop(1, devices, send_owner, 0)
    gather.run(work)

    factors = jnp.dot(
        select_out[...],
        acc_r[:, 2 * rank :].astype(jnp.bfloat16),
        preferred_element_type=jnp.float32,
    ).astype(jnp.bfloat16)
    kd = (
        adapter_scale
        * jnp.dot(factors[:, rank : 2 * rank], up_kv[0], preferred_element_type=jnp.float32)
    ).astype(jnp.bfloat16)
    vd = (
        adapter_scale
        * jnp.dot(factors[:, 2 * rank :], up_kv[1], preferred_element_type=jnp.float32)
    ).astype(jnp.bfloat16)
    for d in range(devices):
        delta_send[d, :, columns:] = jnp.concatenate(
            [kd[:, d * 64 : (d + 1) * 64], vd[:, d * 64 : (d + 1) * 64]], axis=1
        )
    deltas = Exchange(devices, me, delta_send, delta_recv, delta_ssem, delta_rsem)

    def update(device):
        begin = pl.multiple_of(device * columns, columns)
        delta_send[device, :, :columns] = (
            adapter_scale
            * jnp.dot(
                factors[:, :rank],
                up_q[:, pl.ds(begin, columns)],
                preferred_element_type=jnp.float32,
            )
        ).astype(jnp.bfloat16)

    def update_and_send(i, carry):
        device = (me + i) % devices
        update(device)
        deltas.start(device)
        return carry

    lax.fori_loop(1, devices, update_and_send, 0)
    update(me)
    deltas.arrive()
    added = jnp.dot(
        place_out[...],
        delta_recv[...].reshape(devices * capacity, columns + 128),
        preferred_element_type=jnp.float32,
    )
    rows_send[:, :, :columns] = (
        (acc_q[...] + added[:, :columns]).astype(jnp.bfloat16).reshape(devices, rows, columns)
    )
    rows_send[:, :, columns:] = (
        (acc_r[:, : 2 * rank] + added[:, columns:])
        .astype(jnp.bfloat16)
        .reshape(devices, rows, 128)
    )
    exchange = Exchange(devices, me, rows_send, rows_recv, rows_ssem, rows_rsem)
    exchange.start_all()
    gather.finish()
    deltas.finish()
    exchange.arrive()
    for d in range(devices):
        for j in range(columns // HD):
            q_out[:, d * (columns // HD) + j, :] = rows_recv[d, :, j * HD : (j + 1) * HD].astype(
                jnp.float32
            )
    for g in range(KV_HEADS):
        first = rows_recv[2 * g, :, columns:].astype(jnp.float32)
        second = rows_recv[2 * g + 1, :, columns:].astype(jnp.float32)
        k_out[:, g, :] = jnp.concatenate([first[:, :64], second[:, :64]], axis=1)
        v_out[:, g, :] = jnp.concatenate([first[:, 64:], second[:, 64:]], axis=1)
    exchange.finish()


def attend_row(q, k_new, v_new, cosine, sine, visible, cached_k, cached_v):
    heads, size = q.shape
    groups = k_new.shape[0]
    per_group = heads // groups
    scale_factor = 1.0 / math.sqrt(size)

    def turn(x):
        x = x.astype(jnp.float32)
        turned = x * cosine + pltpu.roll(x, size // 2, 1) * sine
        return turned.astype(jnp.bfloat16).astype(jnp.float32)

    def spread(x):
        return jnp.broadcast_to(x[:, None, :], (groups, per_group, size)).reshape(heads, size)

    q_turned = turn(q)
    wide = (heads, groups * size)
    mine = (
        lax.broadcasted_iota(jnp.int32, wide, 0) // per_group
        == lax.broadcasted_iota(jnp.int32, wide, 1) // size
    )
    q_wide = jnp.where(mine, jnp.concatenate([q_turned] * groups, axis=1), 0.0)
    scores = scale_factor * lax.dot_general(
        q_wide.astype(jnp.bfloat16), cached_k, TRANSPOSED, preferred_element_type=jnp.float32
    )
    own_score = scale_factor * jnp.sum(
        q_turned * spread(turn(k_new)), axis=1, keepdims=True
    )
    masked = jnp.where(visible, scores, -1e30)
    largest = jnp.maximum(jnp.max(masked, axis=1, keepdims=True), own_score)
    weights = jnp.where(visible, jnp.exp(masked - largest), 0.0)
    own_weight = jnp.exp(own_score - largest)
    denominator = jnp.sum(weights, axis=1, keepdims=True) + own_weight
    chances = (weights / denominator).astype(jnp.bfloat16)
    own_chance = (own_weight / denominator).astype(jnp.bfloat16).astype(jnp.float32)
    mixed = jnp.dot(chances, cached_v, preferred_element_type=jnp.float32)
    mixed = jnp.concatenate(
        [
            mixed[g * per_group : (g + 1) * per_group, g * size : (g + 1) * size]
            for g in range(groups)
        ],
        axis=0,
    )
    return mixed + own_chance * spread(v_new.astype(jnp.float32))


def output_kernel(
    devices,
    q_ref,
    k_ref,
    v_ref,
    cosine_ref,
    sine_ref,
    length_ref,
    key_cache_ref,
    value_cache_ref,
    place_ref,
    select_ref,
    output_weight_ref,
    down_ref,
    output_up_ref,
    out,
    blocks,
    wo,
    wd,
    up_o,
    acc_o,
    acc_f,
    delta_send,
    delta_recv,
    rows_send,
    rows_recv,
    gather_send,
    gather_recv,
    delta_ssem,
    delta_rsem,
    rows_ssem,
    rows_rsem,
    load_sem,
    cached_k,
    cached_v,
    attended,
):
    me = lax.axis_index("replica")
    rows, heads, size = q_ref.shape
    width = heads * size
    greet_all(devices, me)
    cache_loads = [
        pltpu.make_async_copy(key_cache_ref, cached_k, load_sem.at[3]),
        pltpu.make_async_copy(value_cache_ref, cached_v, load_sem.at[4]),
    ]
    for load in cache_loads:
        load.start()
    chunk = width // CHUNKS
    total = devices * rows
    capacity = 2 * rows
    columns = wo.shape[1]
    loads = [
        pltpu.make_async_copy(output_weight_ref, wo, load_sem.at[0]),
        pltpu.make_async_copy(down_ref.at[0, 3], wd, load_sem.at[1]),
        pltpu.make_async_copy(output_up_ref.at[0], up_o, load_sem.at[2]),
    ]
    for load in loads:
        load.start()
    for load in cache_loads:
        load.wait()
    length = cached_k.shape[1]
    for r in range(rows):
        visible = (
            lax.broadcasted_iota(jnp.int32, (heads, length), 1) < length_ref[r]
        )
        attended[r * heads : (r + 1) * heads, :] = attend_row(
            q_ref[r],
            k_ref[r],
            v_ref[r],
            cosine_ref[r : r + 1, :],
            sine_ref[r : r + 1, :],
            visible,
            cached_k[r],
            cached_v[r],
        )
    chunk_heads = heads // CHUNKS
    for h in range(heads):
        place = h % chunk_heads * size
        blocks[h // chunk_heads, me, :, place : place + size] = attended[
            pl.ds(h, rows, stride=heads), :
        ].astype(jnp.bfloat16)
    await_all(devices)
    gather = Gather(devices, me, blocks, gather_send, gather_recv)

    def work(k):
        if k == 0:
            for load in loads:
                load.wait()
        x = blocks[k].reshape(total, chunk)
        part = pl.ds(k * chunk, chunk)
        o = jnp.dot(x, wo[part, :], preferred_element_type=jnp.float32)
        f = lax.dot_general(x, wd[:, part], TRANSPOSED, preferred_element_type=jnp.float32)
        if k == 0:
            acc_o[...] = o
            acc_f[...] = f
        else:
            acc_o[...] += o
            acc_f[...] += f

    gather.own(0)
    gather.run(work)
    factors = jnp.dot(
        select_ref[...], acc_f[...].astype(jnp.bfloat16), preferred_element_type=jnp.float32
    ).astype(jnp.bfloat16)
    deltas = Exchange(devices, me, delta_send, delta_recv, delta_ssem, delta_rsem)

    def update(device):
        begin = pl.multiple_of(device * columns, columns)
        delta_send[device] = (
            adapter_scale
            * jnp.dot(
                factors, up_o[:, pl.ds(begin, columns)], preferred_element_type=jnp.float32
            )
        ).astype(jnp.bfloat16)

    def update_and_send(i, carry):
        device = (me + i) % devices
        update(device)
        deltas.start(device)
        return carry

    lax.fori_loop(1, devices, update_and_send, 0)
    update(me)
    deltas.arrive()
    added = jnp.dot(
        place_ref[...],
        delta_recv[...].reshape(devices * capacity, columns),
        preferred_element_type=jnp.float32,
    )
    rows_send[...] = (acc_o[...] + added).astype(jnp.bfloat16).reshape(devices, rows, columns)
    exchange = Exchange(devices, me, rows_send, rows_recv, rows_ssem, rows_rsem)
    exchange.start_all()
    gather.finish()
    deltas.finish()
    exchange.arrive()
    for d in range(devices):
        out[:, d * columns : (d + 1) * columns] = rows_recv[d]
    exchange.finish()


def fused(
    hidden,
    input_norm_gain,
    row_adapter_index,
    adapter_slot_table,
    cache_length,
    rotated_key_cache,
    cached_value_table,
    query_weight,
    key_value_weight,
    output_weight,
    adapter_down_weight,
    query_up_weight,
    key_value_up_weight,
    output_up_weight,
):
    devices = lax.axis_size("replica")
    rows, width = hidden.shape
    total, capacity = devices * rows, 2 * rows
    columns = query_weight.shape[1]
    rank = query_up_weight.shape[1]
    bf16, f32 = jnp.bfloat16, jnp.float32
    in_vmem = pl.BlockSpec(memory_space=pltpu.VMEM)
    in_smem = pl.BlockSpec(memory_space=pltpu.SMEM)
    in_any = pl.BlockSpec(memory_space=pl.ANY)
    dma = pltpu.SemaphoreType.DMA
    q_rows, k_rows, v_rows, place, select = pl.pallas_call(
        functools.partial(project_kernel, devices),
        out_shape=(
            jax.ShapeDtypeStruct((rows, HEADS, HD), f32),
            jax.ShapeDtypeStruct((rows, KV_HEADS, HD), f32),
            jax.ShapeDtypeStruct((rows, KV_HEADS, HD), f32),
            jax.ShapeDtypeStruct((total, devices * capacity), bf16),
            jax.ShapeDtypeStruct((capacity, total), bf16),
        ),
        in_specs=[in_vmem] * 2 + [in_smem] * 2 + [in_any] * 5,
        out_specs=(in_vmem,) * 5,
        scratch_shapes=[
            pltpu.VMEM((CHUNKS, devices, rows, width // CHUNKS), bf16),
            pltpu.VMEM((devices, rows, 128), bf16),
            pltpu.VMEM((width, columns), bf16),
            pltpu.VMEM((5, rank, width), bf16),
            pltpu.VMEM((rank, width), bf16),
            pltpu.VMEM(key_value_up_weight.shape[1:], bf16),
            pltpu.VMEM((total, columns), f32),
            pltpu.VMEM((total, 5 * rank), f32),
            pltpu.VMEM((devices, capacity, columns + 128), bf16),
            pltpu.VMEM((devices, capacity, columns + 128), bf16),
            pltpu.VMEM((devices, rows, columns + 128), bf16),
            pltpu.VMEM((devices, rows, columns + 128), bf16),
            dma((CHUNKS, devices)),
            dma((CHUNKS, devices)),
            dma((devices,)),
            dma((devices,)),
            dma((devices,)),
            dma((devices,)),
            dma((devices,)),
            dma((devices,)),
            dma((5,)),
        ],
        compiler_params=pltpu.CompilerParams(
            collective_id=0, has_side_effects=True, vmem_limit_bytes=60 * 2**20
        ),
        name="project",
    )(
        hidden,
        input_norm_gain.reshape(1, width),
        row_adapter_index.reshape(rows),
        adapter_slot_table,
        query_weight,
        key_value_weight,
        adapter_down_weight,
        query_up_weight,
        key_value_up_weight,
    )
    inv_freq = 1000000.0 ** (-(jnp.arange(HD // 2, dtype=f32) * 2.0 / HD))
    angles = cache_length.astype(f32)[:, None] * inv_freq[None, :]
    cosine = jnp.concatenate([jnp.cos(angles), jnp.cos(angles)], axis=-1)
    sine = jnp.concatenate([-jnp.sin(angles), jnp.sin(angles)], axis=-1)
    return pl.pallas_call(
        functools.partial(output_kernel, devices),
        out_shape=jax.ShapeDtypeStruct((rows, width), bf16),
        in_specs=[in_vmem] * 5 + [in_smem] + [in_any] * 2 + [in_vmem] * 2 + [in_any] * 3,
        out_specs=in_vmem,
        scratch_shapes=[
            pltpu.VMEM((CHUNKS, devices, rows, width // CHUNKS), bf16),
            pltpu.VMEM((width, columns), bf16),
            pltpu.VMEM((rank, width), bf16),
            pltpu.VMEM((rank, width), bf16),
            pltpu.VMEM((total, columns), f32),
            pltpu.VMEM((total, rank), f32),
            pltpu.VMEM((devices, capacity, columns), bf16),
            pltpu.VMEM((devices, capacity, columns), bf16),
            pltpu.VMEM((devices, rows, columns), bf16),
            pltpu.VMEM((devices, rows, columns), bf16),
            dma((CHUNKS, devices)),
            dma((CHUNKS, devices)),
            dma((devices,)),
            dma((devices,)),
            dma((devices,)),
            dma((devices,)),
            dma((5,)),
            pltpu.VMEM(rotated_key_cache.shape, bf16),
            pltpu.VMEM(cached_value_table.shape, bf16),
            pltpu.VMEM((rows * HEADS, HD), f32),
        ],
        compiler_params=pltpu.CompilerParams(
            collective_id=1, has_side_effects=True, vmem_limit_bytes=60 * 2**20
        ),
        name="output",
    )(
        q_rows,
        k_rows,
        v_rows,
        cosine,
        sine,
        cache_length,
        rotated_key_cache,
        cached_value_table,
        place,
        select,
        output_weight,
        adapter_down_weight,
        output_up_weight,
    )


def solution(mesh):
    in_specs = (
        P(("group", "replica"), None),
        P(),
        P(("group", "replica"), None),
        P(),
        P(("group", "replica")),
        P(("group", "replica"), None, None),
        P(("group", "replica"), None, None),
        P(None, "replica"),
        P(None, "replica", None),
        P(None, "replica"),
        P("replica", None, None, None),
        P("replica", None, None),
        P("replica", None, None, None),
        P("replica", None, None),
    )
    out_specs = P(("group", "replica"), None)
    body = fused if mesh.shape["replica"] == 16 else local
    return jax.shard_map(body, mesh=mesh, in_specs=in_specs, out_specs=out_specs, check_vma=False)
```
